32 devices in a mesh: wide: 8 (over z, y), narrow: 4 (over x, core).
Axes of the slice: x: 2, y: 2, z: 4, core: 2. Of those that a mesh axis runs over, the one named last changes fastest.
Arguments:
- tiles: float32 [8, 24, 256, 256], P('wide', 'narrow'), may hold values from -12 to 12, as said below
- tile_rows: int32 [8, 24], P('wide', 'narrow'), may hold values from 0 to 31, as said below
- tile_cols: int32 [8, 24], P('wide', 'narrow'), may hold values from 0 to 31, as said below
- tile_counts: int32 [8, 4], P('wide', 'narrow'), may hold values from 0 to 6, as said below
Outputs:
- scaled_tiles: float32 [8, 24, 256, 256], P('wide', 'narrow')
- scaling: float32 [32, 256], P('wide')
The draws below stay inside these ranges and needn't reach their ends.
Inputs may be any that keep to these rules, and one draw needn't show every extreme that they name: `tile_rows`: A live slot of device (w, n) names a block row in w * 4 to (w + 1) * 4 - 1, and every block row has exactly one live diagonal tile, on the device whose block columns hold it. Unused slots name block row w * 4. `tile_cols`: A live slot of device (w, n) names a block column in n * 8 to (n + 1) * 8 - 1, not below its block row; no tile is stored twice. Unused slots name block column n * 8. `tile_counts`: the device that holds a block row's diagonal tile uses all slots. Diagonal tiles are symmetric with diagonal entries in 0.3 to 1.5.
All inputs are finite; a program needn't handle non-finite values.
Results may differ from the reference program's by a relative error of at most 0.00002.
Values sent between devices are 32-bit elements; how exact they have to be, the bound alone decides.
No kernel may reach another device: no remote copies, remote signals or barrier semaphores. Data moves between devices by JAX's collectives and lax.ppermute only.
A program may use at most 64 MiB of HBM per device.

```python
import jax
import jax.numpy as jnp
from jax import lax

TILE = 256
ROWB = 4
ITERS = 2
WGROUPS = 8
NGROUPS = 4
NB = 32
CB = 8
CAP = 6


def structure(key):
    base_key = jax.random.fold_in(key, 11)
    key_count, key_far, key_home = jax.random.split(base_key, 3)
    wide_ids = jnp.arange(WGROUPS).astype(jnp.int32)[:, None]
    narrow_ids = jnp.arange(NGROUPS).astype(jnp.int32)[None, :]
    home_group = wide_ids * ROWB // CB
    extra_count = jax.random.randint(key_count, (WGROUPS, NGROUPS), 0, CAP + 1)
    counts = jnp.where(narrow_ids == home_group, CAP, jnp.where(narrow_ids > home_group, extra_count, 0)).astype(jnp.int32)
    pair_total = ROWB * CB
    far_score = jax.random.randint(key_far, (WGROUPS, NGROUPS, pair_total), 0, 1 << 20) * pair_total + jnp.arange(pair_total)
    far_order = jnp.argsort(far_score, axis=-1)[..., :CAP].astype(jnp.int32)
    far_rows = wide_ids[..., None] * ROWB + far_order // CB
    far_cols = narrow_ids[..., None] * CB + far_order % CB
    upper_row, upper_col = jnp.triu_indices(ROWB, 1)
    upper_total = ROWB * (ROWB - 1) // 2
    home_score = jax.random.randint(key_home, (WGROUPS, upper_total), 0, 1 << 20) * upper_total + jnp.arange(upper_total)
    picked = jnp.argsort(home_score, axis=-1)[:, :CAP - ROWB]
    diag_ids = wide_ids * ROWB + jnp.arange(ROWB).astype(jnp.int32)[None, :]
    home_rows = jnp.concatenate([diag_ids, wide_ids * ROWB + upper_row.astype(jnp.int32)[picked]], axis=1)
    home_cols = jnp.concatenate([diag_ids, wide_ids * ROWB + upper_col.astype(jnp.int32)[picked]], axis=1)
    is_home = (narrow_ids == home_group)[..., None]
    rows = jnp.where(is_home, home_rows[:, None, :], far_rows)
    cols = jnp.where(is_home, home_cols[:, None, :], far_cols)
    live_slots = jnp.arange(CAP)[None, None, :] < counts[..., None]
    rows = jnp.where(live_slots, rows, wide_ids[..., None] * ROWB)
    cols = jnp.where(live_slots, cols, narrow_ids[..., None] * CB)
    return (rows.reshape(WGROUPS, NGROUPS * CAP).astype(jnp.int32), cols.reshape(WGROUPS, NGROUPS * CAP).astype(jnp.int32), counts)


def draw_tile_rows(key, part):
    return structure(key)[0]


def draw_tile_cols(key, part):
    return structure(key)[1]


def draw_tile_counts(key, part):
    return structure(key)[2]


def draw_tiles(key, part):
    rows, cols, counts = structure(key)
    value_key = jax.random.fold_in(key, 23)
    key_base, key_row, key_col, key_tile, key_pivot = jax.random.split(value_key, 5)
    shape = (WGROUPS, NGROUPS * CAP, TILE, TILE)
    base = jax.random.normal(key_base, shape, jnp.float32)
    spread = 1.2
    row_log = jax.random.uniform(key_row, shape[:3], jnp.float32, -spread, spread)
    col_log = jax.random.uniform(key_col, shape[:3], jnp.float32, -spread, spread)
    tile_log = jax.random.uniform(key_tile, shape[:2], jnp.float32, -0.8, 0.8)
    diagonal_tile = rows == cols
    col_log = jnp.where(diagonal_tile[..., None], row_log, col_log)
    matrix = base * jnp.exp(row_log)[..., :, None] * jnp.exp(col_log)[..., None, :] * jnp.exp(tile_log)[..., None, None]
    symmetric = 0.5 * (matrix + jnp.swapaxes(matrix, -1, -2))
    matrix = jnp.where(diagonal_tile[..., None, None], symmetric, matrix)
    pivots = jax.random.uniform(key_pivot, shape[:3], jnp.float32, 0.3, 1.5)
    identity = jnp.eye(TILE, dtype=bool)
    matrix = jnp.where(diagonal_tile[..., None, None] & identity, pivots[..., :, None], matrix)
    return jnp.clip(matrix, -12.0, 12.0)


def setup_inputs(seed: int = 0) -> dict:
    keys = jax.random.split(jax.random.key(seed), 5)
    tiles = draw_tiles(jax.random.fold_in(keys[4], 71), 0)
    tile_rows = draw_tile_rows(jax.random.fold_in(keys[4], 71), 0)
    tile_cols = draw_tile_cols(jax.random.fold_in(keys[4], 71), 0)
    tile_counts = draw_tile_counts(jax.random.fold_in(keys[4], 71), 0)
    return dict(tiles=tiles, tile_rows=tile_rows, tile_cols=tile_cols, tile_counts=tile_counts)


def reference(tiles, tile_rows, tile_cols, tile_counts):
    group_slots = tile_rows.shape[1]
    slot_cap = group_slots // tile_counts.shape[1]
    slot_index = (jnp.arange(group_slots) % slot_cap).astype(jnp.int32)
    live_slots = slot_index[None, :] < jnp.repeat(tile_counts, slot_cap, axis=1)
    scaling = jnp.ones((NB, TILE), jnp.float32)
    flat_rows = tile_rows.reshape(-1).astype(jnp.int32)
    flat_cols = tile_cols.reshape(-1).astype(jnp.int32)
    for iteration in range(ITERS):

        def per_group(packed):
            matrix, rows_here, cols_here, live_here = packed
            scaled = jnp.abs(matrix) * scaling[rows_here][:, :, None] * scaling[cols_here][:, None, :]
            scaled = jnp.where(live_here[:, None, None], scaled, jnp.float32(0.0))
            return (lax.optimization_barrier(jnp.max(scaled, axis=2)), lax.optimization_barrier(jnp.max(scaled, axis=1)))
        row_peak, col_peak = lax.map(per_group, (tiles, tile_rows, tile_cols, live_slots))
        peak = jnp.zeros((NB, TILE), jnp.float32)
        peak = peak.at[flat_rows].max(row_peak.reshape(-1, TILE))
        peak = peak.at[flat_cols].max(col_peak.reshape(-1, TILE))
        scaling = scaling / jnp.sqrt(peak)

    def finish(packed):
        matrix, rows_here, cols_here, live_here = packed
        scaled = matrix * scaling[rows_here][:, :, None] * scaling[cols_here][:, None, :]
        return jnp.where(live_here[:, None, None], scaled, jnp.float32(0.0))
    scaled_tiles = lax.map(finish, (tiles, tile_rows, tile_cols, live_slots))
    return (scaled_tiles, scaling)
```

```python
import functools

import jax
import jax.numpy as jnp
from jax import lax
from jax.experimental import pallas as pl
from jax.experimental.pallas import tpu as pltpu
from jax.sharding import PartitionSpec as P

ROWB = 4
ITERS = 2
BOTH = ("wide", "narrow")
SMEM = pl.BlockSpec(memory_space=pltpu.SMEM)
VMEM = pl.BlockSpec(memory_space=pltpu.VMEM)
HBM = pl.BlockSpec(memory_space=pltpu.HBM)


def raise_row(peak_ref, index, row):
    peak_ref[pl.ds(index, 1), :] = jnp.maximum(peak_ref[pl.ds(index, 1), :], row)


def lane_max(block):
    half = block.shape[1] // 2
    folded = jnp.maximum(block[:, :half], block[:, half:])
    return jnp.max(folded.T, axis=0, keepdims=True)


def as_column(row, half):
    return jnp.broadcast_to(row, (half, row.shape[1])).T


def first_kernel(rows_ref, cols_ref, count_ref, tiles_ref, held_ref, peak_ref, sems):
    slots = tiles_ref.shape[1]
    copies = [
        pltpu.make_async_copy(tiles_ref.at[0, s], held_ref.at[s], sems.at[s])
        for s in range(slots)
    ]
    for copy in copies:
        copy.start()
    peak_ref[...] = jnp.zeros_like(peak_ref)
    for s in range(slots):
        copies[s].wait()

        @pl.when(s < count_ref[0, 0])
        def _():
            size = jnp.abs(held_ref[s])
            raise_row(peak_ref, cols_ref[0, s], jnp.max(size, axis=0, keepdims=True))
            raise_row(peak_ref, rows_ref[0, s], lane_max(size))


def next_kernel(rows_ref, cols_ref, count_ref, held_ref, *refs):
    *old_refs, peak_ref, scale_ref = refs
    slots, _, tile = held_ref.shape
    half = tile // 2
    scale = lax.rsqrt(old_refs[0][...])
    for old_ref in old_refs[1:]:
        scale = scale * lax.rsqrt(old_ref[...])
    scale_ref[...] = scale
    peak_ref[...] = jnp.zeros_like(peak_ref)
    for s in range(slots):

        @pl.when(s < count_ref[0, 0])
        def _():
            size = jnp.abs(held_ref[s])
            row, col = rows_ref[0, s], cols_ref[0, s]
            left = scale_ref[pl.ds(row, 1), :]
            right = scale_ref[pl.ds(col, 1), :]
            raise_row(peak_ref, row, lane_max(size * right) * left)
            column = as_column(left, half)
            below = jnp.concatenate(
                [
                    jnp.max(size[:, :half] * column, axis=0, keepdims=True),
                    jnp.max(size[:, half:] * column, axis=0, keepdims=True),
                ],
                axis=1,
            )
            raise_row(peak_ref, col, below * right)


def last_kernel(row_blocks, rows_ref, cols_ref, count_ref, held_ref, *refs):
    *old_refs, out_ref, own_ref, scale_ref, done_ref, sems = refs
    slots, _, tile = held_ref.shape
    half = tile // 2
    scale = lax.rsqrt(old_refs[0][...])
    for old_ref in old_refs[1:]:
        scale = scale * lax.rsqrt(old_ref[...])
    scale_ref[...] = scale
    start = lax.axis_index("wide") * row_blocks
    for k in range(row_blocks):
        own_ref[pl.ds(k, 1), :] = scale_ref[pl.ds(start + k, 1), :]
    copies = []
    for s in range(slots):
        live = s < count_ref[0, 0]

        @pl.when(live)
        def _():
            left = scale_ref[pl.ds(rows_ref[0, s], 1), :]
            right = scale_ref[pl.ds(cols_ref[0, s], 1), :]
            column = as_column(left, half)
            done_ref[s, :, :half] = held_ref[s, :, :half] * column * right[:, :half]
            done_ref[s, :, half:] = held_ref[s, :, half:] * column * right[:, half:]

        @pl.when(jnp.logical_not(live))
        def _():
            done_ref[s] = jnp.zeros((tile, tile), jnp.float32)

        copy = pltpu.make_async_copy(done_ref.at[s], out_ref.at[0, s], sems.at[s])
        copy.start()
        copies.append(copy)
    for copy in copies:
        copy.wait()


def swap(values, wide_size, narrow_size, wide_bit, narrow_bit, odd_only):
    pairs = []
    for w in range(wide_size):
        for n in range(narrow_size):
            here = w * narrow_size + n
            there = (w ^ wide_bit) * narrow_size + (n ^ narrow_bit)
            pairs.append((here, here if odd_only and n % 2 == 0 else there))
    return jnp.maximum(values, lax.ppermute(values, BOTH, pairs))


def max_over_devices(values, wide_size, narrow_size):
    step = functools.partial(swap, wide_size=wide_size, narrow_size=narrow_size)
    values = step(values, wide_bit=0, narrow_bit=1, odd_only=False)
    steps = []
    bit = 1
    while bit < wide_size:
        steps.append((bit, 0))
        bit *= 2
    bit = 2
    while bit < narrow_size:
        steps.insert(len(steps) - 1, (0, bit))
        bit *= 2
    for wide_bit, narrow_bit in steps:
        values = step(values, wide_bit=wide_bit, narrow_bit=narrow_bit, odd_only=True)
    return step(values, wide_bit=0, narrow_bit=1, odd_only=False)


def on_device(wide_size, narrow_size, row_blocks, tiles, tile_rows, tile_cols, tile_counts):
    slots, tile = tiles.shape[1], tiles.shape[2]
    blocks = row_blocks * wide_size
    places = (tile_rows, tile_cols, tile_counts)
    held_shape = jax.ShapeDtypeStruct((slots, tile, tile), jnp.float32)
    peak_shape = jax.ShapeDtypeStruct((blocks, tile), jnp.float32)
    held, part = pl.pallas_call(
        first_kernel,
        out_shape=(held_shape, peak_shape),
        in_specs=[SMEM] * 3 + [HBM],
        out_specs=(VMEM, VMEM),
        scratch_shapes=[pltpu.SemaphoreType.DMA((slots,))],
        name="first_peaks",
    )(*places, tiles)
    peaks = []
    for iteration in range(ITERS):
        if iteration:
            part = pl.pallas_call(
                next_kernel,
                out_shape=peak_shape,
                in_specs=[SMEM] * 3 + [VMEM] * (1 + len(peaks)),
                out_specs=VMEM,
                scratch_shapes=[pltpu.VMEM((blocks, tile), jnp.float32)],
                name="next_peaks",
            )(*places, held, *peaks)
        peaks.append(max_over_devices(part, wide_size, narrow_size))
    return pl.pallas_call(
        functools.partial(last_kernel, row_blocks),
        out_shape=(
            jax.ShapeDtypeStruct(tiles.shape, jnp.float32),
            jax.ShapeDtypeStruct((row_blocks, tile), jnp.float32),
        ),
        in_specs=[SMEM] * 3 + [VMEM] * (1 + len(peaks)),
        out_specs=(HBM, VMEM),
        scratch_shapes=[
            pltpu.VMEM((blocks, tile), jnp.float32),
            pltpu.VMEM((slots, tile, tile), jnp.float32),
            pltpu.SemaphoreType.DMA((slots,)),
        ],
        name="scaled_tiles",
    )(*places, held, *peaks)


def solution(mesh):
    wide_size, narrow_size = mesh.shape["wide"], mesh.shape["narrow"]
    placed = (
        P("wide", "narrow", None, None),
        P("wide", "narrow"),
        P("wide", "narrow"),
        P("wide", "narrow"),
    )
    row_blocks = ROWB
    return jax.shard_map(
        functools.partial(on_device, wide_size, narrow_size, row_blocks),
        mesh=mesh,
        in_specs=placed,
        out_specs=(P("wide", "narrow", None, None), P("wide", None)),
        check_vma=False,
    )
```

```python
import functools

import jax
import jax.numpy as jnp
from jax import lax
from jax.experimental import pallas as pl
from jax.experimental.pallas import tpu as pltpu
from jax.sharding import PartitionSpec as P

ROWB = 4
ITERS = 2
PARAMS = pltpu.CompilerParams(vmem_limit_bytes=16 << 20)
BOTH = ("wide", "narrow")
SMEM = pl.BlockSpec(memory_space=pltpu.SMEM)
VMEM = pl.BlockSpec(memory_space=pltpu.VMEM)
HBM = pl.BlockSpec(memory_space=pltpu.HBM)


def raise_row(peak_ref, index, row):
    peak_ref[pl.ds(index, 1), :] = jnp.maximum(peak_ref[pl.ds(index, 1), :], row)


def lane_max(block):
    half = block.shape[1] // 2
    folded = jnp.maximum(block[:, :half], block[:, half:])
    return jnp.max(folded.T, axis=0, keepdims=True)


def as_column(row, half):
    return jnp.broadcast_to(row, (half, row.shape[1])).T


def first_kernel(rows_ref, cols_ref, count_ref, tiles_ref, held_ref, peak_ref, sems):
    slots = tiles_ref.shape[1]
    copies = [
        pltpu.make_async_copy(tiles_ref.at[0, s], held_ref.at[s], sems.at[s])
        for s in range(slots)
    ]
    for copy in copies:
        copy.start()
    peak_ref[...] = jnp.zeros_like(peak_ref)
    for s in range(slots):
        copies[s].wait()

        @pl.when(s < count_ref[0, 0])
        def _():
            size = jnp.abs(held_ref[s])
            raise_row(peak_ref, cols_ref[0, s], jnp.max(size, axis=0, keepdims=True))
            raise_row(peak_ref, rows_ref[0, s], lane_max(size))


def next_kernel(rows_ref, cols_ref, count_ref, held_ref, *refs):
    *old_refs, peak_ref, scale_ref = refs
    slots, _, tile = held_ref.shape
    half = tile // 2
    scale = lax.rsqrt(old_refs[0][...])
    for old_ref in old_refs[1:]:
        scale = scale * lax.rsqrt(old_ref[...])
    scale_ref[...] = scale
    peak_ref[...] = jnp.zeros_like(peak_ref)
    for s in range(slots):

        @pl.when(s < count_ref[0, 0])
        def _():
            size = jnp.abs(held_ref[s])
            row, col = rows_ref[0, s], cols_ref[0, s]
            left = scale_ref[pl.ds(row, 1), :]
            right = scale_ref[pl.ds(col, 1), :]
            raise_row(peak_ref, row, lane_max(size * right) * left)
            column = as_column(left, half)
            below = jnp.concatenate(
                [
                    jnp.max(size[:, :half] * column, axis=0, keepdims=True),
                    jnp.max(size[:, half:] * column, axis=0, keepdims=True),
                ],
                axis=1,
            )
            raise_row(peak_ref, col, below * right)


def last_kernel(row_blocks, rows_ref, cols_ref, count_ref, held_ref, *refs):
    *old_refs, out_ref, own_ref, scale_ref, done_ref, sems = refs
    slots, _, tile = held_ref.shape
    half = tile // 2
    scale = lax.rsqrt(old_refs[0][...])
    for old_ref in old_refs[1:]:
        scale = scale * lax.rsqrt(old_ref[...])
    scale_ref[...] = scale
    start = lax.axis_index("wide") * row_blocks
    for k in range(row_blocks):
        own_ref[pl.ds(k, 1), :] = scale_ref[pl.ds(start + k, 1), :]
    copies = []
    for s in range(slots):
        live = s < count_ref[0, 0]

        @pl.when(live)
        def _():
            left = scale_ref[pl.ds(rows_ref[0, s], 1), :]
            right = scale_ref[pl.ds(cols_ref[0, s], 1), :]
            column = as_column(left, half)
            done_ref[s, :, :half] = held_ref[s, :, :half] * column * right[:, :half]
            done_ref[s, :, half:] = held_ref[s, :, half:] * column * right[:, half:]

        @pl.when(jnp.logical_not(live))
        def _():
            done_ref[s] = jnp.zeros((tile, tile), jnp.float32)

        copy = pltpu.make_async_copy(done_ref.at[s], out_ref.at[0, s], sems.at[s])
        copy.start()
        copies.append(copy)
    for copy in copies:
        copy.wait()


def swap(values, wide_size, narrow_size, wide_bit, narrow_bit):
    pairs = []
    for w in range(wide_size):
        for n in range(narrow_size):
            there = (w ^ wide_bit) * narrow_size + (n ^ narrow_bit)
            pairs.append((w * narrow_size + n, there))
    return jnp.maximum(values, lax.ppermute(values, BOTH, pairs))


def max_over_devices(values, wide_size, narrow_size):
    values = swap(values, wide_size, narrow_size, 0, 1)
    steps = []
    bit = 1
    while bit < wide_size:
        steps.append((bit, 1))
        bit *= 2
    bit = 2
    while bit < narrow_size:
        steps.insert(len(steps) - 1, (0, bit + 1))
        bit *= 2
    for wide_bit, narrow_bit in steps:
        values = swap(values, wide_size, narrow_size, wide_bit, narrow_bit)
    return values


def on_device(wide_size, narrow_size, row_blocks, tiles, tile_rows, tile_cols, tile_counts):
    slots, tile = tiles.shape[1], tiles.shape[2]
    blocks = row_blocks * wide_size
    places = (tile_rows, tile_cols, tile_counts)
    held_shape = jax.ShapeDtypeStruct((slots, tile, tile), jnp.float32)
    peak_shape = jax.ShapeDtypeStruct((blocks, tile), jnp.float32)
    held, part = pl.pallas_call(
        first_kernel,
        out_shape=(held_shape, peak_shape),
        in_specs=[SMEM] * 3 + [HBM],
        out_specs=(VMEM, VMEM),
        scratch_shapes=[pltpu.SemaphoreType.DMA((slots,))],
        compiler_params=PARAMS,
        name="first_peaks",
    )(*places, tiles)
    peaks = []
    for iteration in range(ITERS):
        if iteration:
            part = pl.pallas_call(
                next_kernel,
                out_shape=peak_shape,
                in_specs=[SMEM] * 3 + [VMEM] * (1 + len(peaks)),
                out_specs=VMEM,
                scratch_shapes=[pltpu.VMEM((blocks, tile), jnp.float32)],
                compiler_params=PARAMS,
                name="next_peaks",
            )(*places, held, *peaks)
        peaks.append(max_over_devices(part, wide_size, narrow_size))
    return pl.pallas_call(
        functools.partial(last_kernel, row_blocks),
        out_shape=(
            jax.ShapeDtypeStruct(tiles.shape, jnp.float32),
            jax.ShapeDtypeStruct((row_blocks, tile), jnp.float32),
        ),
        in_specs=[SMEM] * 3 + [VMEM] * (1 + len(peaks)),
        out_specs=(HBM, VMEM),
        scratch_shapes=[
            pltpu.VMEM((blocks, tile), jnp.float32),
            pltpu.VMEM((slots, tile, tile), jnp.float32),
            pltpu.SemaphoreType.DMA((slots,)),
        ],
        compiler_params=PARAMS,
        name="scaled_tiles",
    )(*places, held, *peaks)


def solution(mesh):
    wide_size, narrow_size = mesh.shape["wide"], mesh.shape["narrow"]
    placed = (
        P("wide", "narrow", None, None),
        P("wide", "narrow"),
        P("wide", "narrow"),
        P("wide", "narrow"),
    )
    row_blocks = ROWB
    return jax.shard_map(
        functools.partial(on_device, wide_size, narrow_size, row_blocks),
        mesh=mesh,
        in_specs=placed,
        out_specs=(P("wide", "narrow", None, None), P("wide", None)),
        check_vma=False,
    )
```

```python
import functools

import jax
import jax.numpy as jnp
from jax import lax
from jax.experimental import pallas as pl
from jax.experimental.pallas import tpu as pltpu
from jax.sharding import PartitionSpec as P

ROWB = 4
ITERS = 2
PARAMS = pltpu.CompilerParams(vmem_limit_bytes=16 << 20)
BOTH = ("wide", "narrow")
SMEM = pl.BlockSpec(memory_space=pltpu.SMEM)
VMEM = pl.BlockSpec(memory_space=pltpu.VMEM)
HBM = pl.BlockSpec(memory_space=pltpu.HBM)


def kept(values, space):
    return [pltpu.with_memory_space_constraint(value, space) for value in values]


def raise_row(peak_ref, index, row):
    peak_ref[pl.ds(index, 1), :] = jnp.maximum(peak_ref[pl.ds(index, 1), :], row)


def lane_max(block):
    half = block.shape[1] // 2
    folded = jnp.maximum(block[:, :half], block[:, half:])
    return jnp.max(folded.T, axis=0, keepdims=True)


def as_column(row, half):
    return jnp.broadcast_to(row, (half, row.shape[1])).T


def scale_of(old_refs):
    scale = lax.rsqrt(old_refs[0][...])
    for old_ref in old_refs[1:]:
        scale = scale * lax.rsqrt(old_ref[...])
    return scale


def first_kernel(
    count_ref, rows_in, cols_in, tiles_ref, rows_ref, cols_ref, held_ref, peak_ref, sems
):
    slots = tiles_ref.shape[1]
    moves = [(rows_in, rows_ref), (cols_in, cols_ref)]
    moves += [(tiles_ref.at[0, s], held_ref.at[s]) for s in range(slots)]
    copies = [
        pltpu.make_async_copy(source, target, sems.at[k])
        for k, (source, target) in enumerate(moves)
    ]
    for copy in copies:
        copy.start()
    peak_ref[...] = jnp.zeros_like(peak_ref)
    for copy in copies[:2]:
        copy.wait()
    for s in range(slots):
        copies[2 + s].wait()
        live = s < count_ref[0, 0]
        size = jnp.abs(held_ref[s])
        column_max = jnp.max(size, axis=0, keepdims=True)
        raise_row(peak_ref, cols_ref[0, s], jnp.where(live, column_max, 0.0))
        raise_row(peak_ref, rows_ref[0, s], jnp.where(live, lane_max(size), 0.0))


def next_kernel(rows_ref, cols_ref, count_ref, held_ref, *refs):
    *old_refs, peak_ref, scale_ref = refs
    slots, _, tile = held_ref.shape
    half = tile // 2
    scale_ref[...] = scale_of(old_refs)
    peak_ref[...] = jnp.zeros_like(peak_ref)
    for s in range(slots):
        live = s < count_ref[0, 0]
        size = jnp.abs(held_ref[s])
        row, col = rows_ref[0, s], cols_ref[0, s]
        left = scale_ref[pl.ds(row, 1), :]
        right = scale_ref[pl.ds(col, 1), :]
        raise_row(peak_ref, row, jnp.where(live, lane_max(size * right) * left, 0.0))
        column = as_column(left, half)
        below = jnp.concatenate(
            [
                jnp.max(size[:, :half] * column, axis=0, keepdims=True),
                jnp.max(size[:, half:] * column, axis=0, keepdims=True),
            ],
            axis=1,
        )
        raise_row(peak_ref, col, jnp.where(live, below * right, 0.0))


def last_kernel(row_blocks, rows_ref, cols_ref, count_ref, held_ref, *refs):
    *old_refs, out_ref, own_out, scale_ref, own_ref, done_ref, sems = refs
    slots, _, tile = held_ref.shape
    half = tile // 2
    scale_ref[...] = scale_of(old_refs)
    start = lax.axis_index("wide") * row_blocks
    for k in range(row_blocks):
        own_ref[pl.ds(k, 1), :] = scale_ref[pl.ds(start + k, 1), :]
    copies = [pltpu.make_async_copy(own_ref, own_out, sems.at[slots])]
    copies[0].start()
    for s in range(slots):
        live = s < count_ref[0, 0]
        left = scale_ref[pl.ds(rows_ref[0, s], 1), :]
        right = scale_ref[pl.ds(cols_ref[0, s], 1), :]
        column = as_column(left, half)
        for part in (slice(0, half), slice(half, tile)):
            scaled = held_ref[s, :, part] * column * right[:, part]
            done_ref[s, :, part] = jnp.where(live, scaled, 0.0)
        copies.append(pltpu.make_async_copy(done_ref.at[s], out_ref.at[0, s], sems.at[s]))
        copies[-1].start()
    for copy in copies:
        copy.wait()


def swap(values, wide_size, narrow_size, wide_bit, narrow_bit):
    pairs = []
    for w in range(wide_size):
        for n in range(narrow_size):
            there = (w ^ wide_bit) * narrow_size + (n ^ narrow_bit)
            pairs.append((w * narrow_size + n, there))
    return jnp.maximum(values, lax.ppermute(values, BOTH, pairs))


def max_over_devices(values, wide_size, narrow_size):
    values = swap(values, wide_size, narrow_size, 0, 1)
    steps = []
    bit = 1
    while bit < wide_size:
        steps.append((bit, 1))
        bit *= 2
    bit = 2
    while bit < narrow_size:
        steps.insert(len(steps) - 1, (0, bit + 1))
        bit *= 2
    for wide_bit, narrow_bit in steps:
        values = swap(values, wide_size, narrow_size, wide_bit, narrow_bit)
    return values


def on_device(wide_size, narrow_size, tiles, tile_rows, tile_cols, tile_counts):
    slots, tile = tiles.shape[1], tiles.shape[2]
    blocks = ROWB * wide_size
    rows, cols, held, part = pl.pallas_call(
        first_kernel,
        out_shape=(
            pltpu.SMEM(tile_rows.shape, jnp.int32),
            pltpu.SMEM(tile_cols.shape, jnp.int32),
            pltpu.VMEM((slots, tile, tile), jnp.float32),
            pltpu.VMEM((blocks, tile), jnp.float32),
        ),
        in_specs=[SMEM, HBM, HBM, HBM],
        out_specs=(SMEM, SMEM, VMEM, VMEM),
        scratch_shapes=[pltpu.SemaphoreType.DMA((2 + slots,))],
        compiler_params=PARAMS,
        name="first_peaks",
    )(tile_counts, *kept((tile_rows, tile_cols, tiles), pltpu.HBM))
    places = (*kept((rows, cols), pltpu.SMEM), tile_counts)
    held = kept([held], pltpu.VMEM)
    peaks = []
    for iteration in range(ITERS):
        if iteration:
            part = pl.pallas_call(
                next_kernel,
                out_shape=pltpu.VMEM((blocks, tile), jnp.float32),
                in_specs=[SMEM] * 3 + [VMEM] * (1 + len(peaks)),
                out_specs=VMEM,
                scratch_shapes=[pltpu.VMEM((blocks, tile), jnp.float32)],
                compiler_params=PARAMS,
                name="next_peaks",
            )(*places, *held, *peaks)
        full = max_over_devices(part, wide_size, narrow_size)
        peaks += kept([full], pltpu.VMEM)
    return pl.pallas_call(
        functools.partial(last_kernel, ROWB),
        out_shape=(
            jax.ShapeDtypeStruct(tiles.shape, jnp.float32),
            jax.ShapeDtypeStruct((ROWB, tile), jnp.float32),
        ),
        in_specs=[SMEM] * 3 + [VMEM] * (1 + len(peaks)),
        out_specs=(HBM, HBM),
        scratch_shapes=[
            pltpu.VMEM((blocks, tile), jnp.float32),
            pltpu.VMEM((ROWB, tile), jnp.float32),
            pltpu.VMEM((slots, tile, tile), jnp.float32),
            pltpu.SemaphoreType.DMA((slots + 1,)),
        ],
        compiler_params=PARAMS,
        name="scaled_tiles",
    )(*places, *held, *peaks)


def solution(mesh):
    wide_size, narrow_size = mesh.shape["wide"], mesh.shape["narrow"]
    placed = (
        P("wide", "narrow", None, None),
        P("wide", "narrow"),
        P("wide", "narrow"),
        P("wide", "narrow"),
    )
    return jax.shard_map(
        functools.partial(on_device, wide_size, narrow_size),
        mesh=mesh,
        in_specs=placed,
        out_specs=(P("wide", "narrow", None, None), P("wide", None)),
        check_vma=False,
    )
```

```python
import functools

import jax
import jax.numpy as jnp
from jax import lax
from jax.experimental import pallas as pl
from jax.experimental.pallas import tpu as pltpu
from jax.sharding import PartitionSpec as P

ROWB = 4
ITERS = 2
PARAMS = pltpu.CompilerParams(vmem_limit_bytes=16 << 20)
BOTH = ("wide", "narrow")
SMEM = pl.BlockSpec(memory_space=pltpu.SMEM)
VMEM = pl.BlockSpec(memory_space=pltpu.VMEM)
HBM = pl.BlockSpec(memory_space=pltpu.HBM)


def kept(values, space):
    return [pltpu.with_memory_space_constraint(value, space) for value in values]


def raise_row(peak_ref, index, row):
    peak_ref[pl.ds(index, 1), :] = jnp.maximum(peak_ref[pl.ds(index, 1), :], row)


def lane_max(block):
    half = block.shape[1] // 2
    folded = jnp.maximum(block[:, :half], block[:, half:])
    return jnp.max(folded.T, axis=0, keepdims=True)


def as_column(row, half):
    return jnp.broadcast_to(row, (half, row.shape[1])).T


def first_kernel(
    count_ref, rows_in, cols_in, tiles_ref, rows_ref, cols_ref, held_ref, peak_ref, sems
):
    slots = tiles_ref.shape[1]
    moves = [(rows_in, rows_ref), (cols_in, cols_ref)]
    moves += [(tiles_ref.at[0, s], held_ref.at[s]) for s in range(slots)]
    copies = [
        pltpu.make_async_copy(source, target, sems.at[k])
        for k, (source, target) in enumerate(moves)
    ]
    for copy in copies:
        copy.start()
    peak_ref[...] = jnp.zeros_like(peak_ref)
    for copy in copies[:2]:
        copy.wait()
    for s in range(slots):
        copies[2 + s].wait()
        live = s < count_ref[0, 0]
        size = jnp.abs(held_ref[s])
        column_max = jnp.max(size, axis=0, keepdims=True)
        raise_row(peak_ref, cols_ref[0, s], jnp.where(live, column_max, 0.0))
        raise_row(peak_ref, rows_ref[0, s], jnp.where(live, lane_max(size), 0.0))


def next_kernel(rows_ref, cols_ref, count_ref, held_ref, old_ref, peak_ref, scale_ref):
    slots, _, tile = held_ref.shape
    half = tile // 2
    scale_ref[...] = lax.rsqrt(old_ref[...])
    peak_ref[...] = jnp.zeros_like(peak_ref)
    for s in range(slots):
        live = s < count_ref[0, 0]
        size = jnp.abs(held_ref[s])
        row, col = rows_ref[0, s], cols_ref[0, s]
        left = scale_ref[pl.ds(row, 1), :]
        right = scale_ref[pl.ds(col, 1), :]
        raise_row(peak_ref, row, jnp.where(live, lane_max(size * right) * left, 0.0))
        column = as_column(left, half)
        below = jnp.concatenate(
            [
                jnp.max(size[:, :half] * column, axis=0, keepdims=True),
                jnp.max(size[:, half:] * column, axis=0, keepdims=True),
            ],
            axis=1,
        )
        raise_row(peak_ref, col, jnp.where(live, below * right, 0.0))
    peak_ref[...] = peak_ref[...] * old_ref[...]


def last_kernel(
    row_blocks,
    rows_ref,
    cols_ref,
    count_ref,
    held_ref,
    old_ref,
    out_ref,
    own_out,
    scale_ref,
    own_ref,
    done_ref,
    sems,
):
    slots, _, tile = held_ref.shape
    half = tile // 2
    scale_ref[...] = lax.rsqrt(old_ref[...])
    start = lax.axis_index("wide") * row_blocks
    for k in range(row_blocks):
        own_ref[pl.ds(k, 1), :] = scale_ref[pl.ds(start + k, 1), :]
    copies = [pltpu.make_async_copy(own_ref, own_out, sems.at[slots])]
    copies[0].start()
    for s in range(slots):
        live = s < count_ref[0, 0]
        left = scale_ref[pl.ds(rows_ref[0, s], 1), :]
        right = scale_ref[pl.ds(cols_ref[0, s], 1), :]
        column = as_column(left, half)
        for part in (slice(0, half), slice(half, tile)):
            scaled = held_ref[s, :, part] * column * right[:, part]
            done_ref[s, :, part] = jnp.where(live, scaled, 0.0)
        copies.append(pltpu.make_async_copy(done_ref.at[s], out_ref.at[0, s], sems.at[s]))
        copies[-1].start()
    for copy in copies:
        copy.wait()


def swap(values, partner, wide_size, narrow_size):
    pairs = []
    for w in range(wide_size):
        for n in range(narrow_size):
            wide, narrow = partner(w, n)
            pairs.append((w * narrow_size + n, wide * narrow_size + narrow))
    return lax.ppermute(values, BOTH, pairs)


def bits(first, last):
    while first < last:
        yield first
        first *= 2


def max_over_devices(values, wide_size, narrow_size):
    steps = [(0, 1)]
    steps += [(bit, 1) for bit in bits(1, wide_size)]
    steps += [(0, bit + 1) for bit in bits(2, narrow_size)]
    for wide_bit, narrow_bit in steps:
        other = swap(
            values, lambda w, n: (w ^ wide_bit, n ^ narrow_bit), wide_size, narrow_size
        )
        values = jnp.maximum(values, other)
    return values


def window_max(values, start, window):
    old = lax.dynamic_slice_in_dim(values, start, window.shape[0], 0)
    return lax.dynamic_update_slice_in_dim(values, jnp.maximum(old, window), start, 0)


def max_over_users(values, wide_size, narrow_size):
    share = wide_size // narrow_size
    for wide_bit in (0, *bits(1, share)):
        other = swap(values, lambda w, n: (w ^ wide_bit, n ^ 1), wide_size, narrow_size)
        values = jnp.maximum(values, other)

    def along_columns(w, n):
        group = w // share
        return (group ^ group >> 1 ^ n >> 1 ^ n) & 1 == 0

    def first(w, n):
        return (w ^ share, n ^ 1) if along_columns(w, n) else (w, n ^ 3)

    def second(w, n):
        return (w ^ 2 * share if along_columns(w, n) else w ^ share, n ^ 1)

    pair = 2 * values.shape[0] // narrow_size
    w, n = lax.axis_index("wide"), lax.axis_index("narrow")
    column_start, row_start = (n >> 1) * pair, (w // (2 * share)) * pair
    chosen = along_columns(w, n)
    start = jnp.where(chosen, column_start, row_start)
    window = lax.dynamic_slice_in_dim(values, start, pair, 0)
    for partner in (first, second):
        window = jnp.maximum(window, swap(window, partner, wide_size, narrow_size))
    other = swap(window, lambda w, n: (w, n ^ 1), wide_size, narrow_size)
    values = window_max(values, start, window)
    return window_max(values, jnp.where(chosen, row_start, column_start), other)


def on_device(wide_size, narrow_size, tiles, tile_rows, tile_cols, tile_counts):
    slots, tile = tiles.shape[1], tiles.shape[2]
    blocks = ROWB * wide_size
    rows, cols, held, part = pl.pallas_call(
        first_kernel,
        out_shape=(
            pltpu.SMEM(tile_rows.shape, jnp.int32),
            pltpu.SMEM(tile_cols.shape, jnp.int32),
            pltpu.VMEM((slots, tile, tile), jnp.float32),
            pltpu.VMEM((blocks, tile), jnp.float32),
        ),
        in_specs=[SMEM, HBM, HBM, HBM],
        out_specs=(SMEM, SMEM, VMEM, VMEM),
        scratch_shapes=[pltpu.SemaphoreType.DMA((2 + slots,))],
        compiler_params=PARAMS,
        name="first_peaks",
    )(tile_counts, *kept((tile_rows, tile_cols, tiles), pltpu.HBM))
    places = (*kept((rows, cols), pltpu.SMEM), tile_counts)
    held = kept([held], pltpu.VMEM)
    for iteration in range(1, ITERS):
        reduce = max_over_users if narrow_size == 4 else max_over_devices
        full = reduce(part, wide_size, narrow_size)
        part = pl.pallas_call(
            next_kernel,
            out_shape=pltpu.VMEM((blocks, tile), jnp.float32),
            in_specs=[SMEM] * 3 + [VMEM] * 2,
            out_specs=VMEM,
            scratch_shapes=[pltpu.VMEM((blocks, tile), jnp.float32)],
            compiler_params=PARAMS,
            name="next_peaks",
        )(*places, *held, *kept([full], pltpu.VMEM))
    full = max_over_devices(part, wide_size, narrow_size)
    return pl.pallas_call(
        functools.partial(last_kernel, ROWB),
        out_shape=(
            jax.ShapeDtypeStruct(tiles.shape, jnp.float32),
            jax.ShapeDtypeStruct((ROWB, tile), jnp.float32),
        ),
        in_specs=[SMEM] * 3 + [VMEM] * 2,
        out_specs=(HBM, HBM),
        scratch_shapes=[
            pltpu.VMEM((blocks, tile), jnp.float32),
            pltpu.VMEM((ROWB, tile), jnp.float32),
            pltpu.VMEM((slots, tile, tile), jnp.float32),
            pltpu.SemaphoreType.DMA((slots + 1,)),
        ],
        compiler_params=PARAMS,
        name="scaled_tiles",
    )(*places, *held, *kept([full], pltpu.VMEM))


def solution(mesh):
    wide_size, narrow_size = mesh.shape["wide"], mesh.shape["narrow"]
    placed = (
        P("wide", "narrow", None, None),
        P("wide", "narrow"),
        P("wide", "narrow"),
        P("wide", "narrow"),
    )
    return jax.shard_map(
        functools.partial(on_device, wide_size, narrow_size),
        mesh=mesh,
        in_specs=placed,
        out_specs=(P("wide", "narrow", None, None), P("wide", None)),
        check_vma=False,
    )
```

```python
import functools

import jax
import jax.numpy as jnp
from jax import lax
from jax.experimental import pallas as pl
from jax.experimental.pallas import tpu as pltpu
from jax.sharding import PartitionSpec as P

ROWB = 4
ITERS = 2
PARAMS = pltpu.CompilerParams(vmem_limit_bytes=16 << 20)
BOTH = ("wide", "narrow")
SMEM = pl.BlockSpec(memory_space=pltpu.SMEM)
VMEM = pl.BlockSpec(memory_space=pltpu.VMEM)
HBM = pl.BlockSpec(memory_space=pltpu.HBM)


def kept(values, space):
    return [pltpu.with_memory_space_constraint(value, space) for value in values]


def raise_row(peak_ref, index, row):
    peak_ref[pl.ds(index, 1), :] = jnp.maximum(peak_ref[pl.ds(index, 1), :], row)


def lane_max(block):
    half = block.shape[1] // 2
    folded = jnp.maximum(block[:, :half], block[:, half:])
    return jnp.max(folded.T, axis=0, keepdims=True)


def as_column(row, half):
    return jnp.broadcast_to(row, (half, row.shape[1])).T


def first_kernel(
    count_ref, rows_in, cols_in, tiles_ref, rows_ref, cols_ref, held_ref, peak_ref, sems
):
    slots = tiles_ref.shape[1]
    moves = [(rows_in, rows_ref), (cols_in, cols_ref)]
    moves += [(tiles_ref.at[0, s], held_ref.at[s]) for s in range(slots)]
    copies = [
        pltpu.make_async_copy(source, target, sems.at[k])
        for k, (source, target) in enumerate(moves)
    ]
    for copy in copies:
        copy.start()
    peak_ref[...] = jnp.zeros_like(peak_ref)
    for copy in copies[:2]:
        copy.wait()
    for s in range(slots):
        copies[2 + s].wait()
        live = s < count_ref[0, 0]
        size = jnp.abs(held_ref[s])
        column_max = jnp.max(size, axis=0, keepdims=True)
        raise_row(peak_ref, cols_ref[0, s], jnp.where(live, column_max, 0.0))
        raise_row(peak_ref, rows_ref[0, s], jnp.where(live, lane_max(size), 0.0))


def next_kernel(rows_ref, cols_ref, count_ref, held_ref, old_ref, peak_ref, scale_ref):
    slots, _, tile = held_ref.shape
    half = tile // 2
    scale_ref[...] = lax.rsqrt(old_ref[...])
    peak_ref[...] = jnp.zeros_like(peak_ref)
    for s in range(slots):
        live = s < count_ref[0, 0]
        size = jnp.abs(held_ref[s])
        row, col = rows_ref[0, s], cols_ref[0, s]
        left = scale_ref[pl.ds(row, 1), :]
        right = scale_ref[pl.ds(col, 1), :]
        raise_row(peak_ref, row, jnp.where(live, lane_max(size * right) * left, 0.0))
        column = as_column(left, half)
        below = jnp.concatenate(
            [
                jnp.max(size[:, :half] * column, axis=0, keepdims=True),
                jnp.max(size[:, half:] * column, axis=0, keepdims=True),
            ],
            axis=1,
        )
        raise_row(peak_ref, col, jnp.where(live, below * right, 0.0))
    peak_ref[...] = peak_ref[...] * old_ref[...]


def last_kernel(
    row_blocks,
    rows_ref,
    cols_ref,
    count_ref,
    held_ref,
    old_ref,
    out_ref,
    own_out,
    scale_ref,
    own_ref,
    done_ref,
    sems,
):
    slots, _, tile = held_ref.shape
    half = tile // 2
    scale_ref[...] = lax.rsqrt(old_ref[...])
    start = lax.axis_index("wide") * row_blocks
    for k in range(row_blocks):
        own_ref[pl.ds(k, 1), :] = scale_ref[pl.ds(start + k, 1), :]
    copies = [pltpu.make_async_copy(own_ref, own_out, sems.at[slots])]
    copies[0].start()
    for s in range(slots):
        live = s < count_ref[0, 0]
        left = scale_ref[pl.ds(rows_ref[0, s], 1), :]
        right = scale_ref[pl.ds(cols_ref[0, s], 1), :]
        column = as_column(left, half)
        for part in (slice(0, half), slice(half, tile)):
            scaled = held_ref[s, :, part] * column * right[:, part]
            done_ref[s, :, part] = jnp.where(live, scaled, 0.0)
        copies.append(pltpu.make_async_copy(done_ref.at[s], out_ref.at[0, s], sems.at[s]))
        copies[-1].start()
    for copy in copies:
        copy.wait()


def swap(values, partner, wide_size, narrow_size):
    pairs = []
    for w in range(wide_size):
        for n in range(narrow_size):
            wide, narrow = partner(w, n)
            pairs.append((w * narrow_size + n, wide * narrow_size + narrow))
    return lax.ppermute(values, BOTH, pairs)


def bits(first, last):
    while first < last:
        yield first
        first *= 2


def max_over_devices(values, wide_size, narrow_size):
    steps = [(0, 1)]
    steps += [(bit, 1) for bit in bits(1, wide_size)]
    steps += [(0, bit + 1) for bit in bits(2, narrow_size)]
    for wide_bit, narrow_bit in steps:
        other = swap(
            values, lambda w, n: (w ^ wide_bit, n ^ narrow_bit), wide_size, narrow_size
        )
        values = jnp.maximum(values, other)
    return values


def window_max(values, start, window):
    old = lax.dynamic_slice_in_dim(values, start, window.shape[0], 0)
    return lax.dynamic_update_slice_in_dim(values, jnp.maximum(old, window), start, 0)


def swap_in_chip(values, wide_size, narrow_size):
    columns = values.shape[0] // narrow_size
    row_start = lax.axis_index("wide") * ROWB
    n = lax.axis_index("narrow")
    sent = jnp.concatenate(
        [
            lax.dynamic_slice_in_dim(values, n * columns, columns, 0),
            lax.dynamic_slice_in_dim(values, row_start, ROWB, 0),
        ]
    )
    other = swap(sent, lambda w, n: (w, n ^ 1), wide_size, narrow_size)
    values = window_max(values, (n ^ 1) * columns, other[:columns])
    return window_max(values, row_start, other[columns:])


def windows(values, wide_size, narrow_size):
    size = 2 * values.shape[0] // narrow_size
    columns = (lax.axis_index("narrow") >> 1) * size
    rows = lax.axis_index("wide") // (2 * wide_size // narrow_size) * size
    return columns, rows, size


def max_over_users(values, wide_size, narrow_size):
    share = wide_size // narrow_size

    def along_columns(w, n):
        lane = n ^ n >> 1
        for bit in bits(1, wide_size):
            lane = lane ^ w // bit
        return lane & 1 == 0

    def first(w, n):
        return (w ^ share, n ^ 1) if along_columns(w, n) else (w, n ^ 3)

    def second(w, n):
        return (w ^ 2 * share if along_columns(w, n) else w ^ share, n ^ 1)

    values = swap_in_chip(values, wide_size, narrow_size)
    columns, rows, size = windows(values, wide_size, narrow_size)
    chosen = along_columns(lax.axis_index("wide"), lax.axis_index("narrow"))
    start = jnp.where(chosen, columns, rows)
    window = lax.dynamic_slice_in_dim(values, start, size, 0)
    for bit in bits(1, share):
        other = swap(window, lambda w, n: (w ^ bit, n ^ 1), wide_size, narrow_size)
        window = jnp.maximum(window, other)
    for partner in (first, second):
        window = jnp.maximum(window, swap(window, partner, wide_size, narrow_size))
    other = swap(window, lambda w, n: (w, n ^ 1), wide_size, narrow_size)
    values = window_max(values, start, window)
    return window_max(values, jnp.where(chosen, rows, columns), other)


def max_of_rows_too(values, wide_size, narrow_size):
    values = swap_in_chip(values, wide_size, narrow_size)
    for bit in bits(1, wide_size // 2):
        other = swap(values, lambda w, n: (w ^ bit, n ^ 1), wide_size, narrow_size)
        values = jnp.maximum(values, other)
    columns, rows, size = windows(values, wide_size, narrow_size)
    for start, partner in (
        (columns, lambda w, n: (w ^ wide_size // 2, n ^ 1)),
        (rows, lambda w, n: (w, n ^ 3)),
    ):
        window = lax.dynamic_slice_in_dim(values, start, size, 0)
        other = swap(window, partner, wide_size, narrow_size)
        values = window_max(values, start, other)
    return values


def on_device(wide_size, narrow_size, tiles, tile_rows, tile_cols, tile_counts):
    slots, tile = tiles.shape[1], tiles.shape[2]
    blocks = ROWB * wide_size
    four = narrow_size == 4
    rows, cols, held, part = pl.pallas_call(
        first_kernel,
        out_shape=(
            pltpu.SMEM(tile_rows.shape, jnp.int32),
            pltpu.SMEM(tile_cols.shape, jnp.int32),
            pltpu.VMEM((slots, tile, tile), jnp.float32),
            pltpu.VMEM((blocks, tile), jnp.float32),
        ),
        in_specs=[SMEM, HBM, HBM, HBM],
        out_specs=(SMEM, SMEM, VMEM, VMEM),
        scratch_shapes=[pltpu.SemaphoreType.DMA((2 + slots,))],
        compiler_params=PARAMS,
        name="first_peaks",
    )(tile_counts, *kept((tile_rows, tile_cols, tiles), pltpu.HBM))
    places = (*kept((rows, cols), pltpu.SMEM), tile_counts)
    held = kept([held], pltpu.VMEM)
    for iteration in range(1, ITERS):
        full = (max_over_users if four else max_over_devices)(part, wide_size, narrow_size)
        part = pl.pallas_call(
            next_kernel,
            out_shape=pltpu.VMEM((blocks, tile), jnp.float32),
            in_specs=[SMEM] * 3 + [VMEM] * 2,
            out_specs=VMEM,
            scratch_shapes=[pltpu.VMEM((blocks, tile), jnp.float32)],
            compiler_params=PARAMS,
            name="next_peaks",
        )(*places, *held, *kept([full], pltpu.VMEM))
    full = (max_of_rows_too if four else max_over_devices)(part, wide_size, narrow_size)
    return pl.pallas_call(
        functools.partial(last_kernel, ROWB),
        out_shape=(
            jax.ShapeDtypeStruct(tiles.shape, jnp.float32),
            jax.ShapeDtypeStruct((ROWB, tile), jnp.float32),
        ),
        in_specs=[SMEM] * 3 + [VMEM] * 2,
        out_specs=(HBM, HBM),
        scratch_shapes=[
            pltpu.VMEM((blocks, tile), jnp.float32),
            pltpu.VMEM((ROWB, tile), jnp.float32),
            pltpu.VMEM((slots, tile, tile), jnp.float32),
            pltpu.SemaphoreType.DMA((slots + 1,)),
        ],
        compiler_params=PARAMS,
        name="scaled_tiles",
    )(*places, *held, *kept([full], pltpu.VMEM))


def solution(mesh):
    wide_size, narrow_size = mesh.shape["wide"], mesh.shape["narrow"]
    placed = (
        P("wide", "narrow", None, None),
        P("wide", "narrow"),
        P("wide", "narrow"),
        P("wide", "narrow"),
    )
    return jax.shard_map(
        functools.partial(on_device, wide_size, narrow_size),
        mesh=mesh,
        in_specs=placed,
        out_specs=(P("wide", "narrow", None, None), P("wide", None)),
        check_vma=False,
    )
```

```python
import functools

import jax
import jax.numpy as jnp
from jax import lax
from jax.experimental import pallas as pl
from jax.experimental.pallas import tpu as pltpu
from jax.sharding import PartitionSpec as P

ROWB = 4
ITERS = 2
PARAMS = pltpu.CompilerParams(vmem_limit_bytes=16 << 20)
BOTH = ("wide", "narrow")
SMEM = pl.BlockSpec(memory_space=pltpu.SMEM)
VMEM = pl.BlockSpec(memory_space=pltpu.VMEM)
HBM = pl.BlockSpec(memory_space=pltpu.HBM)


def kept(values, space):
    return [pltpu.with_memory_space_constraint(value, space) for value in values]


def raise_row(peak_ref, index, row):
    peak_ref[pl.ds(index, 1), :] = jnp.maximum(peak_ref[pl.ds(index, 1), :], row)


def lane_max(block):
    half = block.shape[1] // 2
    folded = jnp.maximum(block[:, :half], block[:, half:])
    return jnp.max(folded.T, axis=0, keepdims=True)


def as_column(row, half):
    return jnp.broadcast_to(row, (half, row.shape[1])).T


def first_kernel(
    count_ref, rows_in, cols_in, tiles_ref, rows_ref, cols_ref, held_ref, peak_ref, sems
):
    slots = tiles_ref.shape[1]
    moves = [(rows_in, rows_ref), (cols_in, cols_ref)]
    moves += [(tiles_ref.at[0, s], held_ref.at[s]) for s in range(slots)]
    copies = [
        pltpu.make_async_copy(source, target, sems.at[k])
        for k, (source, target) in enumerate(moves)
    ]
    for copy in copies:
        copy.start()
    peak_ref[...] = jnp.zeros_like(peak_ref)
    for copy in copies[:2]:
        copy.wait()
    for first in range(0, slots, 2):
        found = []
        for copy in copies[2 + first : 4 + first]:
            copy.wait()
        for s in range(first, min(first + 2, slots)):
            size = jnp.abs(held_ref[s])
            found.append((s, jnp.max(size, axis=0, keepdims=True), lane_max(size)))
        for s, column_max, row_max in found:
            live = s < count_ref[0, 0]
            raise_row(peak_ref, cols_ref[0, s], jnp.where(live, column_max, 0.0))
            raise_row(peak_ref, rows_ref[0, s], jnp.where(live, row_max, 0.0))


def next_kernel(rows_ref, cols_ref, count_ref, held_ref, old_ref, peak_ref, scale_ref):
    slots, _, tile = held_ref.shape
    half = tile // 2
    scale_ref[...] = lax.rsqrt(old_ref[...])
    peak_ref[...] = jnp.zeros_like(peak_ref)
    found = []
    for s in range(slots):
        size = jnp.abs(held_ref[s])
        left = scale_ref[pl.ds(rows_ref[0, s], 1), :]
        right = scale_ref[pl.ds(cols_ref[0, s], 1), :]
        row_max = lane_max(size * right) * left
        column = as_column(left, half)
        below = jnp.concatenate(
            [
                jnp.max(size[:, :half] * column, axis=0, keepdims=True),
                jnp.max(size[:, half:] * column, axis=0, keepdims=True),
            ],
            axis=1,
        )
        found.append((row_max, below * right))
    for s, (row_max, column_max) in enumerate(found):
        live = s < count_ref[0, 0]
        raise_row(peak_ref, rows_ref[0, s], jnp.where(live, row_max, 0.0))
        raise_row(peak_ref, cols_ref[0, s], jnp.where(live, column_max, 0.0))
    peak_ref[...] = peak_ref[...] * old_ref[...]


def last_kernel(
    row_blocks,
    rows_ref,
    cols_ref,
    count_ref,
    held_ref,
    old_ref,
    out_ref,
    own_out,
    scale_ref,
    own_ref,
    done_ref,
    sems,
):
    slots, _, tile = held_ref.shape
    half = tile // 2
    scale_ref[...] = lax.rsqrt(old_ref[...])
    start = lax.axis_index("wide") * row_blocks
    for k in range(row_blocks):
        own_ref[pl.ds(k, 1), :] = scale_ref[pl.ds(start + k, 1), :]
    copies = [pltpu.make_async_copy(own_ref, own_out, sems.at[slots])]
    copies[0].start()
    for s in range(slots):
        live = s < count_ref[0, 0]
        left = scale_ref[pl.ds(rows_ref[0, s], 1), :]
        right = scale_ref[pl.ds(cols_ref[0, s], 1), :]
        column = as_column(left, half)
        for part in (slice(0, half), slice(half, tile)):
            scaled = held_ref[s, :, part] * column * right[:, part]
            done_ref[s, :, part] = jnp.where(live, scaled, 0.0)
        copies.append(pltpu.make_async_copy(done_ref.at[s], out_ref.at[0, s], sems.at[s]))
        copies[-1].start()
    for copy in copies:
        copy.wait()


def swap(values, partner, wide_size, narrow_size):
    pairs = []
    for w in range(wide_size):
        for n in range(narrow_size):
            wide, narrow = partner(w, n)
            pairs.append((w * narrow_size + n, wide * narrow_size + narrow))
    return lax.ppermute(values, BOTH, pairs)


def bits(first, last):
    while first < last:
        yield first
        first *= 2


def max_over_devices(values, wide_size, narrow_size):
    steps = [(0, 1)]
    steps += [(bit, 1) for bit in bits(1, wide_size)]
    steps += [(0, bit + 1) for bit in bits(2, narrow_size)]
    for wide_bit, narrow_bit in steps:
        other = swap(
            values, lambda w, n: (w ^ wide_bit, n ^ narrow_bit), wide_size, narrow_size
        )
        values = jnp.maximum(values, other)
    return values


def window_max(values, start, window):
    old = lax.dynamic_slice_in_dim(values, start, window.shape[0], 0)
    return lax.dynamic_update_slice_in_dim(values, jnp.maximum(old, window), start, 0)


def swap_in_chip(values, wide_size, narrow_size):
    columns = values.shape[0] // narrow_size
    row_start = lax.axis_index("wide") * ROWB
    n = lax.axis_index("narrow")
    sent = jnp.concatenate(
        [
            lax.dynamic_slice_in_dim(values, n * columns, columns, 0),
            lax.dynamic_slice_in_dim(values, row_start, ROWB, 0),
        ]
    )
    other = swap(sent, lambda w, n: (w, n ^ 1), wide_size, narrow_size)
    values = window_max(values, (n ^ 1) * columns, other[:columns])
    return window_max(values, row_start, other[columns:])


def windows(values, wide_size, narrow_size):
    size = 2 * values.shape[0] // narrow_size
    columns = (lax.axis_index("narrow") >> 1) * size
    rows = lax.axis_index("wide") // (2 * wide_size // narrow_size) * size
    return columns, rows, size


def max_over_users(values, wide_size, narrow_size):
    share = wide_size // narrow_size

    def along_columns(w, n):
        lane = n ^ n >> 1
        for bit in bits(1, wide_size):
            lane = lane ^ w // bit
        return lane & 1 == 0

    def first(w, n):
        return (w ^ share, n ^ 1) if along_columns(w, n) else (w, n ^ 3)

    def second(w, n):
        return (w ^ 2 * share if along_columns(w, n) else w ^ share, n ^ 1)

    values = swap_in_chip(values, wide_size, narrow_size)
    columns, rows, size = windows(values, wide_size, narrow_size)
    chosen = along_columns(lax.axis_index("wide"), lax.axis_index("narrow"))
    start = jnp.where(chosen, columns, rows)
    window = lax.dynamic_slice_in_dim(values, start, size, 0)
    for bit in bits(1, share):
        other = swap(window, lambda w, n: (w ^ bit, n ^ 1), wide_size, narrow_size)
        window = jnp.maximum(window, other)
    for partner in (first, second):
        window = jnp.maximum(window, swap(window, partner, wide_size, narrow_size))
    other = swap(window, lambda w, n: (w, n ^ 1), wide_size, narrow_size)
    values = window_max(values, start, window)
    return window_max(values, jnp.where(chosen, rows, columns), other)


def max_of_rows_too(values, wide_size, narrow_size):
    values = swap_in_chip(values, wide_size, narrow_size)
    columns, rows, size = windows(values, wide_size, narrow_size)
    share, group_size = wide_size // narrow_size, size // 2
    group = lax.axis_index("wide") // share
    for bit in bits(1, wide_size // 2):
        group_start = (group if bit < share else group | 1) * group_size
        sent = jnp.concatenate(
            [
                lax.dynamic_slice_in_dim(values, columns, size, 0),
                lax.dynamic_slice_in_dim(values, group_start, group_size, 0),
            ]
        )
        other = swap(sent, lambda w, n: (w ^ bit, n ^ 1), wide_size, narrow_size)
        values = window_max(values, columns, other[:size])
        values = window_max(values, group_start, other[size:])
    for start, partner in (
        (columns, lambda w, n: (w ^ wide_size // 2, n ^ 1)),
        (rows, lambda w, n: (w, n ^ 3)),
    ):
        window = lax.dynamic_slice_in_dim(values, start, size, 0)
        other = swap(window, partner, wide_size, narrow_size)
        values = window_max(values, start, other)
    return values


def on_device(wide_size, narrow_size, tiles, tile_rows, tile_cols, tile_counts):
    slots, tile = tiles.shape[1], tiles.shape[2]
    blocks = ROWB * wide_size
    four = narrow_size == 4
    rows, cols, held, part = pl.pallas_call(
        first_kernel,
        out_shape=(
            pltpu.SMEM(tile_rows.shape, jnp.int32),
            pltpu.SMEM(tile_cols.shape, jnp.int32),
            pltpu.VMEM((slots, tile, tile), jnp.float32),
            pltpu.VMEM((blocks, tile), jnp.float32),
        ),
        in_specs=[SMEM, HBM, HBM, HBM],
        out_specs=(SMEM, SMEM, VMEM, VMEM),
        scratch_shapes=[pltpu.SemaphoreType.DMA((2 + slots,))],
        compiler_params=PARAMS,
        name="first_peaks",
    )(tile_counts, *kept((tile_rows, tile_cols, tiles), pltpu.HBM))
    places = (*kept((rows, cols), pltpu.SMEM), tile_counts)
    held = kept([held], pltpu.VMEM)
    for iteration in range(1, ITERS):
        full = (max_over_users if four else max_over_devices)(part, wide_size, narrow_size)
        part = pl.pallas_call(
            next_kernel,
            out_shape=pltpu.VMEM((blocks, tile), jnp.float32),
            in_specs=[SMEM] * 3 + [VMEM] * 2,
            out_specs=VMEM,
            scratch_shapes=[pltpu.VMEM((blocks, tile), jnp.float32)],
            compiler_params=PARAMS,
            name="next_peaks",
        )(*places, *held, *kept([full], pltpu.VMEM))
    full = (max_of_rows_too if four else max_over_devices)(part, wide_size, narrow_size)
    return pl.pallas_call(
        functools.partial(last_kernel, ROWB),
        out_shape=(
            jax.ShapeDtypeStruct(tiles.shape, jnp.float32),
            jax.ShapeDtypeStruct((ROWB, tile), jnp.float32),
        ),
        in_specs=[SMEM] * 3 + [VMEM] * 2,
        out_specs=(HBM, HBM),
        scratch_shapes=[
            pltpu.VMEM((blocks, tile), jnp.float32),
            pltpu.VMEM((ROWB, tile), jnp.float32),
            pltpu.VMEM((slots, tile, tile), jnp.float32),
            pltpu.SemaphoreType.DMA((slots + 1,)),
        ],
        compiler_params=PARAMS,
        name="scaled_tiles",
    )(*places, *held, *kept([full], pltpu.VMEM))


def solution(mesh):
    wide_size, narrow_size = mesh.shape["wide"], mesh.shape["narrow"]
    placed = (
        P("wide", "narrow", None, None),
        P("wide", "narrow"),
        P("wide", "narrow"),
        P("wide", "narrow"),
    )
    return jax.shard_map(
        functools.partial(on_device, wide_size, narrow_size),
        mesh=mesh,
        in_specs=placed,
        out_specs=(P("wide", "narrow", None, None), P("wide", None)),
        check_vma=False,
    )
```

```python
import functools

import jax
import jax.numpy as jnp
from jax import lax
from jax.experimental import pallas as pl
from jax.experimental.pallas import tpu as pltpu
from jax.sharding import PartitionSpec as P

ROWB = 4
ITERS = 2
PARAMS = pltpu.CompilerParams(vmem_limit_bytes=16 << 20)
BOTH = ("wide", "narrow")
SMEM = pl.BlockSpec(memory_space=pltpu.SMEM)
VMEM = pl.BlockSpec(memory_space=pltpu.VMEM)
HBM = pl.BlockSpec(memory_space=pltpu.HBM)


def kept(values, space):
    return [pltpu.with_memory_space_constraint(value, space) for value in values]


def raise_row(peak_ref, index, row):
    peak_ref[pl.ds(index, 1), :] = jnp.maximum(peak_ref[pl.ds(index, 1), :], row)


def lane_max(block):
    half = block.shape[1] // 2
    folded = jnp.maximum(block[:, :half], block[:, half:])
    return jnp.max(folded.T, axis=0, keepdims=True)


def as_column(row, half):
    return jnp.broadcast_to(row, (half, row.shape[1])).T


def first_kernel(
    count_ref,
    rows_in,
    cols_in,
    tiles_ref,
    rows_ref,
    cols_ref,
    held_ref,
    peak_ref,
    places_ref,
    sems,
):
    slots = tiles_ref.shape[1]
    moves = [(rows_in, rows_ref), (cols_in, cols_ref)]
    moves += [(tiles_ref.at[0, s], held_ref.at[s]) for s in range(slots)]
    copies = [
        pltpu.make_async_copy(source, target, sems.at[k])
        for k, (source, target) in enumerate(moves)
    ]
    for copy in copies:
        copy.start()
    peak_ref[...] = jnp.zeros_like(peak_ref)
    for copy in copies[:2]:
        copy.wait()
    values = [count_ref[0, 0]]
    values += [ref[0, s] for s in range(slots) for ref in (rows_ref, cols_ref)]
    lane = lax.broadcasted_iota(jnp.int32, places_ref.shape, 1)
    places = jnp.zeros(places_ref.shape, jnp.int32)
    for k, value in enumerate(values):
        places = jnp.where(lane == k, value, places)
    places_ref[...] = places.astype(jnp.float32)
    for first in range(0, slots, 2):
        found = []
        for copy in copies[2 + first : 4 + first]:
            copy.wait()
        for s in range(first, min(first + 2, slots)):
            size = jnp.abs(held_ref[s])
            found.append((s, jnp.max(size, axis=0, keepdims=True), lane_max(size)))
        for s, column_max, row_max in found:
            live = s < count_ref[0, 0]
            raise_row(peak_ref, cols_ref[0, s], jnp.where(live, column_max, 0.0))
            raise_row(peak_ref, rows_ref[0, s], jnp.where(live, row_max, 0.0))


def places_kernel(index_ref, places_ref, whole_ref, sem):
    whole_ref[...] = index_ref[...].astype(jnp.int32)
    copy = pltpu.make_async_copy(whole_ref, places_ref, sem.at[0])
    copy.start()
    copy.wait()


def next_kernel(
    rows_ref, cols_ref, count_ref, mate_places, held_ref, mate_ref, old_ref, peak_ref, scale_ref
):
    slots, _, tile = held_ref.shape
    half = tile // 2
    scale_ref[...] = lax.rsqrt(old_ref[...])
    peak_ref[...] = jnp.zeros_like(peak_ref)

    def add(tiles_ref, count, places):
        found = []
        for s, (row, col) in enumerate(places):
            size = jnp.abs(tiles_ref[s])
            left = scale_ref[pl.ds(row, 1), :]
            right = scale_ref[pl.ds(col, 1), :]
            row_max = lane_max(size * right) * left
            column = as_column(left, half)
            below = jnp.concatenate(
                [
                    jnp.max(size[:, :half] * column, axis=0, keepdims=True),
                    jnp.max(size[:, half:] * column, axis=0, keepdims=True),
                ],
                axis=1,
            )
            found.append((row_max, below * right))
        for s, (row_max, column_max) in enumerate(found):
            raise_row(peak_ref, places[s][0], jnp.where(s < count, row_max, 0.0))
            raise_row(peak_ref, places[s][1], jnp.where(s < count, column_max, 0.0))

    given = [mate_places[0, k] for k in range(2 * slots + 1)]
    own = [(rows_ref[0, s], cols_ref[0, s]) for s in range(slots)]
    add(held_ref, count_ref[0, 0], own)
    add(mate_ref, given[0], list(zip(given[1::2], given[2::2])))
    peak_ref[...] = peak_ref[...] * old_ref[...]


def last_kernel(
    row_blocks,
    rows_ref,
    cols_ref,
    count_ref,
    held_ref,
    old_ref,
    out_ref,
    own_out,
    scale_ref,
    own_ref,
    done_ref,
    sems,
):
    slots, _, tile = held_ref.shape
    half = tile // 2
    scale_ref[...] = lax.rsqrt(old_ref[...])
    start = lax.axis_index("wide") * row_blocks
    for k in range(row_blocks):
        own_ref[pl.ds(k, 1), :] = scale_ref[pl.ds(start + k, 1), :]
    copies = [pltpu.make_async_copy(own_ref, own_out, sems.at[slots])]
    copies[0].start()
    for s in range(slots):
        live = s < count_ref[0, 0]
        left = scale_ref[pl.ds(rows_ref[0, s], 1), :]
        right = scale_ref[pl.ds(cols_ref[0, s], 1), :]
        column = as_column(left, half)
        for part in (slice(0, half), slice(half, tile)):
            scaled = held_ref[s, :, part] * column * right[:, part]
            done_ref[s, :, part] = jnp.where(live, scaled, 0.0)
        copies.append(pltpu.make_async_copy(done_ref.at[s], out_ref.at[0, s], sems.at[s]))
        copies[-1].start()
    for copy in copies:
        copy.wait()


def swap(values, partner, wide_size, narrow_size):
    pairs = []
    for w in range(wide_size):
        for n in range(narrow_size):
            wide, narrow = partner(w, n)
            pairs.append((w * narrow_size + n, wide * narrow_size + narrow))
    return lax.ppermute(values, BOTH, pairs)


def bits(first, last):
    while first < last:
        yield first
        first *= 2


def max_over_chips(values, wide_size, narrow_size):
    steps = [(bit, 1) for bit in bits(1, wide_size)]
    steps += [(0, bit + 1) for bit in bits(2, narrow_size)]
    for wide_bit, narrow_bit in steps:
        other = swap(
            values, lambda w, n: (w ^ wide_bit, n ^ narrow_bit), wide_size, narrow_size
        )
        values = jnp.maximum(values, other)
    return values


def window_max(values, start, window):
    old = lax.dynamic_slice_in_dim(values, start, window.shape[0], 0)
    return lax.dynamic_update_slice_in_dim(values, jnp.maximum(old, window), start, 0)


def swap_in_chip(values, places, wide_size, narrow_size):
    columns = values.shape[0] // narrow_size
    row_start = lax.axis_index("wide") * ROWB
    n = lax.axis_index("narrow")
    sent = jnp.concatenate(
        [
            lax.dynamic_slice_in_dim(values, n * columns, columns, 0),
            lax.dynamic_slice_in_dim(values, row_start, ROWB, 0),
            places,
        ]
    )
    other = swap(sent, lambda w, n: (w, n ^ 1), wide_size, narrow_size)
    values = window_max(values, (n ^ 1) * columns, other[:columns])
    return window_max(values, row_start, other[columns:-1]), other[-1:]


def windows(values, wide_size, narrow_size):
    size = 2 * values.shape[0] // narrow_size
    columns = (lax.axis_index("narrow") >> 1) * size
    rows = lax.axis_index("wide") // (2 * wide_size // narrow_size) * size
    return columns, rows, size


def max_over_users(values, wide_size, narrow_size):
    share = wide_size // narrow_size

    def along_columns(w, n):
        lane = n ^ n >> 1
        for bit in bits(1, wide_size):
            lane = lane ^ w // bit
        return lane & 1 == 0

    def first(w, n):
        return (w ^ share, n ^ 1) if along_columns(w, n) else (w, n ^ 3)

    def second(w, n):
        return (w ^ 2 * share if along_columns(w, n) else w ^ share, n ^ 1)

    columns, rows, size = windows(values, wide_size, narrow_size)
    chosen = along_columns(lax.axis_index("wide"), lax.axis_index("narrow"))
    start = jnp.where(chosen, columns, rows)
    window = lax.dynamic_slice_in_dim(values, start, size, 0)
    for bit in bits(1, share):
        other = swap(window, lambda w, n: (w ^ bit, n ^ 1), wide_size, narrow_size)
        window = jnp.maximum(window, other)
    for partner in (first, second):
        window = jnp.maximum(window, swap(window, partner, wide_size, narrow_size))
    other = swap(window, lambda w, n: (w, n ^ 1), wide_size, narrow_size)
    values = window_max(values, start, window)
    return window_max(values, jnp.where(chosen, rows, columns), other)


def max_of_rows_too(values, wide_size, narrow_size):
    columns, rows, size = windows(values, wide_size, narrow_size)
    share, group_size = wide_size // narrow_size, size // 2
    group = lax.axis_index("wide") // share
    for bit in bits(1, wide_size // 2):
        group_start = (group if bit < share else group | 1) * group_size
        sent = jnp.concatenate(
            [
                lax.dynamic_slice_in_dim(values, columns, size, 0),
                lax.dynamic_slice_in_dim(values, group_start, group_size, 0),
            ]
        )
        other = swap(sent, lambda w, n: (w ^ bit, n ^ 1), wide_size, narrow_size)
        values = window_max(values, columns, other[:size])
        values = window_max(values, group_start, other[size:])
    for start, partner in (
        (columns, lambda w, n: (w ^ wide_size // 2, n ^ 1)),
        (rows, lambda w, n: (w, n ^ 3)),
    ):
        window = lax.dynamic_slice_in_dim(values, start, size, 0)
        other = swap(window, partner, wide_size, narrow_size)
        values = window_max(values, start, other)
    return values


def on_device(wide_size, narrow_size, tiles, tile_rows, tile_cols, tile_counts):
    slots, tile = tiles.shape[1], tiles.shape[2]
    blocks = ROWB * wide_size
    four = narrow_size == 4
    rows, cols, held, part, index = pl.pallas_call(
        first_kernel,
        out_shape=(
            pltpu.SMEM(tile_rows.shape, jnp.int32),
            pltpu.SMEM(tile_cols.shape, jnp.int32),
            pltpu.VMEM((slots, tile, tile), jnp.float32),
            pltpu.VMEM((blocks, tile), jnp.float32),
            pltpu.VMEM((1, tile), jnp.float32),
        ),
        in_specs=[SMEM, HBM, HBM, HBM],
        out_specs=(SMEM, SMEM, VMEM, VMEM, VMEM),
        scratch_shapes=[pltpu.SemaphoreType.DMA((2 + slots,))],
        compiler_params=PARAMS,
        name="first_peaks",
    )(tile_counts, *kept((tile_rows, tile_cols, tiles), pltpu.HBM))
    places = (*kept((rows, cols), pltpu.SMEM), tile_counts)
    part, index = swap_in_chip(part, index, wide_size, narrow_size)
    part, sent = lax.optimization_barrier((part, held))
    mate = swap(sent, lambda w, n: (w, n ^ 1), wide_size, narrow_size)
    held = kept([held], pltpu.VMEM)
    mate_places = pl.pallas_call(
        places_kernel,
        out_shape=pltpu.SMEM(index.shape, jnp.int32),
        in_specs=[VMEM],
        out_specs=SMEM,
        scratch_shapes=[pltpu.VMEM(index.shape, jnp.int32), pltpu.SemaphoreType.DMA((1,))],
        compiler_params=PARAMS,
        name="other_places",
    )(*kept([index], pltpu.VMEM))
    places_too = (*places, *kept([mate_places], pltpu.SMEM))
    for iteration in range(1, ITERS):
        full = (max_over_users if four else max_over_chips)(part, wide_size, narrow_size)
        part = pl.pallas_call(
            next_kernel,
            out_shape=pltpu.VMEM((blocks, tile), jnp.float32),
            in_specs=[SMEM] * 4 + [VMEM] * 3,
            out_specs=VMEM,
            scratch_shapes=[pltpu.VMEM((blocks, tile), jnp.float32)],
            compiler_params=PARAMS,
            name="next_peaks",
        )(*places_too, *held, *kept([mate, full], pltpu.VMEM))
    full = (max_of_rows_too if four else max_over_chips)(part, wide_size, narrow_size)
    return pl.pallas_call(
        functools.partial(last_kernel, ROWB),
        out_shape=(
            jax.ShapeDtypeStruct(tiles.shape, jnp.float32),
            jax.ShapeDtypeStruct((ROWB, tile), jnp.float32),
        ),
        in_specs=[SMEM] * 3 + [VMEM] * 2,
        out_specs=(HBM, HBM),
        scratch_shapes=[
            pltpu.VMEM((blocks, tile), jnp.float32),
            pltpu.VMEM((ROWB, tile), jnp.float32),
            pltpu.VMEM((slots, tile, tile), jnp.float32),
            pltpu.SemaphoreType.DMA((slots + 1,)),
        ],
        compiler_params=PARAMS,
        name="scaled_tiles",
    )(*places, *held, *kept([full], pltpu.VMEM))


def solution(mesh):
    wide_size, narrow_size = mesh.shape["wide"], mesh.shape["narrow"]
    placed = (
        P("wide", "narrow", None, None),
        P("wide", "narrow"),
        P("wide", "narrow"),
        P("wide", "narrow"),
    )
    return jax.shard_map(
        functools.partial(on_device, wide_size, narrow_size),
        mesh=mesh,
        in_specs=placed,
        out_specs=(P("wide", "narrow", None, None), P("wide", None)),
        check_vma=False,
    )
```

```python
import functools

import jax
import jax.numpy as jnp
from jax import lax
from jax.experimental import pallas as pl
from jax.experimental.pallas import tpu as pltpu
from jax.sharding import PartitionSpec as P

ROWB = 4
ITERS = 2
PIECE = 2
PARAMS = pltpu.CompilerParams(vmem_limit_bytes=16 << 20)
BOTH = ("wide", "narrow")
SMEM = pl.BlockSpec(memory_space=pltpu.SMEM)
VMEM = pl.BlockSpec(memory_space=pltpu.VMEM)
HBM = pl.BlockSpec(memory_space=pltpu.HBM)


def kept(values, space):
    return [pltpu.with_memory_space_constraint(value, space) for value in values]


def raise_row(peak_ref, index, row):
    peak_ref[pl.ds(index, 1), :] = jnp.maximum(peak_ref[pl.ds(index, 1), :], row)


def lane_max(block):
    half = block.shape[1] // 2
    folded = jnp.maximum(block[:, :half], block[:, half:])
    return jnp.max(folded.T, axis=0, keepdims=True)


def as_column(row, half):
    return jnp.broadcast_to(row, (half, row.shape[1])).T


def first_kernel(
    count_ref,
    rows_in,
    cols_in,
    tiles_ref,
    rows_ref,
    cols_ref,
    peak_ref,
    places_ref,
    *refs,
):
    *held_refs, sems = refs
    slots = tiles_ref.shape[1]
    held = [ref.at[s] for ref in held_refs for s in range(ref.shape[0])]
    moves = [(rows_in, rows_ref), (cols_in, cols_ref)]
    moves += [(tiles_ref.at[0, s], held[s]) for s in range(slots)]
    copies = [
        pltpu.make_async_copy(source, target, sems.at[k])
        for k, (source, target) in enumerate(moves)
    ]
    for copy in copies:
        copy.start()
    peak_ref[...] = jnp.zeros_like(peak_ref)
    for copy in copies[:2]:
        copy.wait()
    values = [count_ref[0, 0]]
    values += [ref[0, s] for s in range(slots) for ref in (rows_ref, cols_ref)]
    lane = lax.broadcasted_iota(jnp.int32, places_ref.shape, 1)
    places = jnp.zeros(places_ref.shape, jnp.int32)
    for k, value in enumerate(values):
        places = jnp.where(lane == k, value, places)
    places_ref[...] = places.astype(jnp.float32)
    for first in range(0, slots, 2):
        found = []
        for copy in copies[2 + first : 4 + first]:
            copy.wait()
        for s in range(first, min(first + 2, slots)):
            size = jnp.abs(held[s][...])
            found.append((s, jnp.max(size, axis=0, keepdims=True), lane_max(size)))
        for s, column_max, row_max in found:
            live = s < count_ref[0, 0]
            raise_row(peak_ref, cols_ref[0, s], jnp.where(live, column_max, 0.0))
            raise_row(peak_ref, rows_ref[0, s], jnp.where(live, row_max, 0.0))


def places_kernel(index_ref, places_ref, whole_ref, sem):
    whole_ref[...] = index_ref[...].astype(jnp.int32)
    copy = pltpu.make_async_copy(whole_ref, places_ref, sem.at[0])
    copy.start()
    copy.wait()


def next_kernel(row_blocks, rows_ref, cols_ref, count_ref, mate_places, old_ref, *refs):
    *tile_refs, peak_ref, scale_ref, column_ref = refs
    tiles = [ref.at[s] for ref in tile_refs for s in range(ref.shape[0])]
    slots, tile = len(tiles) // 2, tiles[0].shape[0]
    half = tile // 2
    scale_ref[...] = lax.rsqrt(old_ref[...])
    peak_ref[...] = jnp.zeros_like(peak_ref)
    start = lax.axis_index("wide") * row_blocks
    for k in range(row_blocks):
        column_ref[k] = as_column(scale_ref[pl.ds(start + k, 1), :], half)

    def add(tiles, count, places):
        found = []
        for tile_ref, (row, col) in zip(tiles, places):
            size = jnp.abs(tile_ref[...])
            left = scale_ref[pl.ds(row, 1), :]
            right = scale_ref[pl.ds(col, 1), :]
            row_max = lane_max(size * right) * left
            column = column_ref[row - start]
            below = jnp.concatenate(
                [
                    jnp.max(size[:, :half] * column, axis=0, keepdims=True),
                    jnp.max(size[:, half:] * column, axis=0, keepdims=True),
                ],
                axis=1,
            )
            found.append((row_max, below * right))
        for s, (row_max, column_max) in enumerate(found):
            raise_row(peak_ref, places[s][0], jnp.where(s < count, row_max, 0.0))
            raise_row(peak_ref, places[s][1], jnp.where(s < count, column_max, 0.0))

    given = [mate_places[0, k] for k in range(2 * slots + 1)]
    own = [(rows_ref[0, s], cols_ref[0, s]) for s in range(slots)]
    add(tiles[:slots], count_ref[0, 0], own)
    add(tiles[slots:], given[0], list(zip(given[1::2], given[2::2])))
    peak_ref[...] = peak_ref[...] * old_ref[...]


def last_kernel(row_blocks, rows_ref, cols_ref, count_ref, old_ref, *refs):
    *held_refs, out_ref, own_out, scale_ref, own_ref, done_ref, sems = refs
    held = [ref.at[s] for ref in held_refs for s in range(ref.shape[0])]
    slots, tile = len(held), held[0].shape[0]
    half = tile // 2
    scale_ref[...] = lax.rsqrt(old_ref[...])
    start = lax.axis_index("wide") * row_blocks
    for k in range(row_blocks):
        own_ref[pl.ds(k, 1), :] = scale_ref[pl.ds(start + k, 1), :]
    copies = [pltpu.make_async_copy(own_ref, own_out, sems.at[slots])]
    copies[0].start()
    for s in range(slots):
        live = s < count_ref[0, 0]
        left = scale_ref[pl.ds(rows_ref[0, s], 1), :]
        right = scale_ref[pl.ds(cols_ref[0, s], 1), :]
        column = as_column(left, half)
        for part in (slice(0, half), slice(half, tile)):
            scaled = held[s][:, part] * column * right[:, part]
            done_ref[s, :, part] = jnp.where(live, scaled, 0.0)
        copies.append(pltpu.make_async_copy(done_ref.at[s], out_ref.at[0, s], sems.at[s]))
        copies[-1].start()
    for copy in copies:
        copy.wait()


def swap(values, partner, wide_size, narrow_size):
    pairs = []
    for w in range(wide_size):
        for n in range(narrow_size):
            wide, narrow = partner(w, n)
            pairs.append((w * narrow_size + n, wide * narrow_size + narrow))
    return lax.ppermute(values, BOTH, pairs)


def bits(first, last):
    while first < last:
        yield first
        first *= 2


def max_over_chips(values, wide_size, narrow_size):
    steps = [(bit, 1) for bit in bits(1, wide_size)]
    steps += [(0, bit + 1) for bit in bits(2, narrow_size)]
    for wide_bit, narrow_bit in steps:
        other = swap(
            values, lambda w, n: (w ^ wide_bit, n ^ narrow_bit), wide_size, narrow_size
        )
        values = jnp.maximum(values, other)
    return values


def window_max(values, start, window):
    old = lax.dynamic_slice_in_dim(values, start, window.shape[0], 0)
    return lax.dynamic_update_slice_in_dim(values, jnp.maximum(old, window), start, 0)


def swap_in_chip(values, places, wide_size, narrow_size):
    columns = values.shape[0] // narrow_size
    row_start = lax.axis_index("wide") * ROWB
    n = lax.axis_index("narrow")
    sent = jnp.concatenate(
        [
            lax.dynamic_slice_in_dim(values, n * columns, columns, 0),
            lax.dynamic_slice_in_dim(values, row_start, ROWB, 0),
            places,
        ]
    )
    other = swap(sent, lambda w, n: (w, n ^ 1), wide_size, narrow_size)
    values = window_max(values, (n ^ 1) * columns, other[:columns])
    return window_max(values, row_start, other[columns:-1]), other[-1:]


def windows(values, wide_size, narrow_size):
    size = 2 * values.shape[0] // narrow_size
    columns = (lax.axis_index("narrow") >> 1) * size
    rows = lax.axis_index("wide") // (2 * wide_size // narrow_size) * size
    return columns, rows, size


def max_over_users(values, wide_size, narrow_size):
    share = wide_size // narrow_size

    def along_columns(w, n):
        lane = n ^ n >> 1
        for bit in bits(1, wide_size):
            lane = lane ^ w // bit
        return lane & 1 == 0

    def first(w, n):
        return (w ^ share, n ^ 1) if along_columns(w, n) else (w, n ^ 3)

    def second(w, n):
        return (w ^ 2 * share if along_columns(w, n) else w ^ share, n ^ 1)

    columns, rows, size = windows(values, wide_size, narrow_size)
    chosen = along_columns(lax.axis_index("wide"), lax.axis_index("narrow"))
    start = jnp.where(chosen, columns, rows)
    window = lax.dynamic_slice_in_dim(values, start, size, 0)
    for bit in bits(1, share):
        other = swap(window, lambda w, n: (w ^ bit, n ^ 1), wide_size, narrow_size)
        window = jnp.maximum(window, other)
    for partner in (first, second):
        window = jnp.maximum(window, swap(window, partner, wide_size, narrow_size))
    other = swap(window, lambda w, n: (w, n ^ 1), wide_size, narrow_size)
    values = window_max(values, start, window)
    return window_max(values, jnp.where(chosen, rows, columns), other)


def max_of_rows_too(values, wide_size, narrow_size):
    columns, rows, size = windows(values, wide_size, narrow_size)
    share, group_size = wide_size // narrow_size, size // 2
    group = lax.axis_index("wide") // share
    for bit in bits(1, wide_size // 2):
        group_start = (group if bit < share else group | 1) * group_size
        sent = jnp.concatenate(
            [
                lax.dynamic_slice_in_dim(values, columns, size, 0),
                lax.dynamic_slice_in_dim(values, group_start, group_size, 0),
            ]
        )
        other = swap(sent, lambda w, n: (w ^ bit, n ^ 1), wide_size, narrow_size)
        values = window_max(values, columns, other[:size])
        values = window_max(values, group_start, other[size:])
    for start, partner in (
        (columns, lambda w, n: (w ^ wide_size // 2, n ^ 1)),
        (rows, lambda w, n: (w, n ^ 3)),
    ):
        window = lax.dynamic_slice_in_dim(values, start, size, 0)
        other = swap(window, partner, wide_size, narrow_size)
        values = window_max(values, start, other)
    return values


def on_device(wide_size, narrow_size, tiles, tile_rows, tile_cols, tile_counts):
    slots, tile = tiles.shape[1], tiles.shape[2]
    blocks = ROWB * wide_size
    four = narrow_size == 4
    sizes = [min(PIECE, slots - s) for s in range(0, slots, PIECE)]
    rows, cols, part, index, *held = pl.pallas_call(
        first_kernel,
        out_shape=(
            pltpu.SMEM(tile_rows.shape, jnp.int32),
            pltpu.SMEM(tile_cols.shape, jnp.int32),
            pltpu.VMEM((blocks, tile), jnp.float32),
            pltpu.VMEM((1, tile), jnp.float32),
            *[pltpu.VMEM((size, tile, tile), jnp.float32) for size in sizes],
        ),
        in_specs=[SMEM, HBM, HBM, HBM],
        out_specs=(SMEM, SMEM, VMEM, VMEM, *[VMEM for size in sizes]),
        scratch_shapes=[pltpu.SemaphoreType.DMA((2 + slots,))],
        compiler_params=PARAMS,
        name="first_peaks",
    )(tile_counts, *kept((tile_rows, tile_cols, tiles), pltpu.HBM))
    places = (*kept((rows, cols), pltpu.SMEM), tile_counts)
    part, index = swap_in_chip(part, index, wide_size, narrow_size)
    part, *sent = lax.optimization_barrier((part, *held))
    mates = [swap(piece, lambda w, n: (w, n ^ 1), wide_size, narrow_size) for piece in sent]
    held = kept(held, pltpu.VMEM)
    mate_places = pl.pallas_call(
        places_kernel,
        out_shape=pltpu.SMEM(index.shape, jnp.int32),
        in_specs=[VMEM],
        out_specs=SMEM,
        scratch_shapes=[pltpu.VMEM(index.shape, jnp.int32), pltpu.SemaphoreType.DMA((1,))],
        compiler_params=PARAMS,
        name="other_places",
    )(*kept([index], pltpu.VMEM))
    places_too = (*places, *kept([mate_places], pltpu.SMEM))
    for iteration in range(1, ITERS):
        full = (max_over_users if four else max_over_chips)(part, wide_size, narrow_size)
        part = pl.pallas_call(
            functools.partial(next_kernel, ROWB),
            out_shape=pltpu.VMEM((blocks, tile), jnp.float32),
            in_specs=[SMEM] * 4 + [VMEM] * (1 + 2 * len(held)),
            out_specs=VMEM,
            scratch_shapes=[
                pltpu.VMEM((blocks, tile), jnp.float32),
                pltpu.VMEM((ROWB, tile, tile // 2), jnp.float32),
            ],
            compiler_params=PARAMS,
            name="next_peaks",
        )(*places_too, *kept([full], pltpu.VMEM), *held, *kept(mates, pltpu.VMEM))
    full = (max_of_rows_too if four else max_over_chips)(part, wide_size, narrow_size)
    return pl.pallas_call(
        functools.partial(last_kernel, ROWB),
        out_shape=(
            jax.ShapeDtypeStruct(tiles.shape, jnp.float32),
            jax.ShapeDtypeStruct((ROWB, tile), jnp.float32),
        ),
        in_specs=[SMEM] * 3 + [VMEM] * (1 + len(held)),
        out_specs=(HBM, HBM),
        scratch_shapes=[
            pltpu.VMEM((blocks, tile), jnp.float32),
            pltpu.VMEM((ROWB, tile), jnp.float32),
            pltpu.VMEM((slots, tile, tile), jnp.float32),
            pltpu.SemaphoreType.DMA((slots + 1,)),
        ],
        compiler_params=PARAMS,
        name="scaled_tiles",
    )(*places, *kept([full], pltpu.VMEM), *held)


def solution(mesh):
    wide_size, narrow_size = mesh.shape["wide"], mesh.shape["narrow"]
    placed = (
        P("wide", "narrow", None, None),
        P("wide", "narrow"),
        P("wide", "narrow"),
        P("wide", "narrow"),
    )
    return jax.shard_map(
        functools.partial(on_device, wide_size, narrow_size),
        mesh=mesh,
        in_specs=placed,
        out_specs=(P("wide", "narrow", None, None), P("wide", None)),
        check_vma=False,
    )
```

```python
import functools

import jax
import jax.numpy as jnp
from jax import lax
from jax.experimental import pallas as pl
from jax.experimental.pallas import tpu as pltpu
from jax.sharding import PartitionSpec as P

ROWB = 4
ITERS = 2
PIECE = 2
PARAMS = pltpu.CompilerParams(vmem_limit_bytes=16 << 20)
BOTH = ("wide", "narrow")
SMEM = pl.BlockSpec(memory_space=pltpu.SMEM)
VMEM = pl.BlockSpec(memory_space=pltpu.VMEM)
HBM = pl.BlockSpec(memory_space=pltpu.HBM)


def kept(values, space):
    return [pltpu.with_memory_space_constraint(value, space) for value in values]


def raise_row(peak_ref, index, row):
    peak_ref[pl.ds(index, 1), :] = jnp.maximum(peak_ref[pl.ds(index, 1), :], row)


def lane_max(block):
    half = block.shape[1] // 2
    folded = jnp.maximum(block[:, :half], block[:, half:])
    return jnp.max(folded.T, axis=0, keepdims=True)


def as_column(row, half):
    return jnp.broadcast_to(row, (half, row.shape[1])).T


def first_kernel(
    count_ref,
    rows_in,
    cols_in,
    tiles_ref,
    rows_ref,
    cols_ref,
    peak_ref,
    places_ref,
    *refs,
):
    *held_refs, sems = refs
    slots = tiles_ref.shape[1]
    held = [ref.at[s] for ref in held_refs for s in range(ref.shape[0])]
    moves = [(rows_in, rows_ref), (cols_in, cols_ref)]
    moves += [(tiles_ref.at[0, s], held[s]) for s in range(slots)]
    copies = [
        pltpu.make_async_copy(source, target, sems.at[k])
        for k, (source, target) in enumerate(moves)
    ]
    for copy in copies:
        copy.start()
    peak_ref[...] = jnp.zeros_like(peak_ref)
    for copy in copies[:2]:
        copy.wait()
    values = [count_ref[0, 0]]
    values += [ref[0, s] for s in range(slots) for ref in (rows_ref, cols_ref)]
    lane = lax.broadcasted_iota(jnp.int32, places_ref.shape, 1)
    places = jnp.zeros(places_ref.shape, jnp.int32)
    for k, value in enumerate(values):
        places = jnp.where(lane == k, value, places)
    places_ref[...] = places.astype(jnp.float32)
    for first in range(0, slots, 2):
        found = []
        for copy in copies[2 + first : 4 + first]:
            copy.wait()
        for s in range(first, min(first + 2, slots)):
            size = jnp.abs(held[s][...])
            found.append((s, jnp.max(size, axis=0, keepdims=True), lane_max(size)))
        for s, column_max, row_max in found:
            live = s < count_ref[0, 0]
            raise_row(peak_ref, cols_ref[0, s], jnp.where(live, column_max, 0.0))
            raise_row(peak_ref, rows_ref[0, s], jnp.where(live, row_max, 0.0))


def places_kernel(index_ref, places_ref, whole_ref, sem):
    whole_ref[...] = index_ref[...].astype(jnp.int32)
    copy = pltpu.make_async_copy(whole_ref, places_ref, sem.at[0])
    copy.start()
    copy.wait()


def next_kernel(row_blocks, rows_ref, cols_ref, count_ref, mate_places, old_ref, *refs):
    *tile_refs, peak_ref, scale_ref, column_ref = refs
    tiles = [ref.at[s] for ref in tile_refs for s in range(ref.shape[0])]
    slots, tile = len(tiles) // 2, tiles[0].shape[0]
    half = tile // 2
    scale_ref[...] = lax.rsqrt(old_ref[...])
    peak_ref[...] = jnp.zeros_like(peak_ref)
    start = lax.axis_index("wide") * row_blocks
    for k in range(row_blocks):
        column_ref[k] = as_column(scale_ref[pl.ds(start + k, 1), :], half)

    def add(tiles, count, places):
        found = []
        for tile_ref, (row, col) in zip(tiles, places):
            size = jnp.abs(tile_ref[...])
            left = scale_ref[pl.ds(row, 1), :]
            right = scale_ref[pl.ds(col, 1), :]
            row_max = lane_max(size * right) * left
            column = column_ref[row - start]
            below = jnp.concatenate(
                [
                    jnp.max(size[:, :half] * column, axis=0, keepdims=True),
                    jnp.max(size[:, half:] * column, axis=0, keepdims=True),
                ],
                axis=1,
            )
            found.append((row_max, below * right))
        for s, (row_max, column_max) in enumerate(found):
            raise_row(peak_ref, places[s][0], jnp.where(s < count, row_max, 0.0))
            raise_row(peak_ref, places[s][1], jnp.where(s < count, column_max, 0.0))

    given = [mate_places[0, k] for k in range(2 * slots + 1)]
    own = [(rows_ref[0, s], cols_ref[0, s]) for s in range(slots)]
    add(tiles[:slots], count_ref[0, 0], own)
    add(tiles[slots:], given[0], list(zip(given[1::2], given[2::2])))
    peak_ref[...] = peak_ref[...] * old_ref[...]


def last_kernel(rows_ref, cols_ref, count_ref, old_ref, *refs):
    *held_refs, out_ref, scale_ref, done_ref, sems = refs
    held = [ref.at[s] for ref in held_refs for s in range(ref.shape[0])]
    slots, tile = len(held), held[0].shape[0]
    half = tile // 2
    scale_ref[...] = lax.rsqrt(old_ref[...])
    copies = []
    for s in range(slots):
        live = s < count_ref[0, 0]
        left = scale_ref[pl.ds(rows_ref[0, s], 1), :]
        right = scale_ref[pl.ds(cols_ref[0, s], 1), :]
        column = as_column(left, half)
        for part in (slice(0, half), slice(half, tile)):
            scaled = held[s][:, part] * column * right[:, part]
            done_ref[s, :, part] = jnp.where(live, scaled, 0.0)
        copies.append(pltpu.make_async_copy(done_ref.at[s], out_ref.at[0, s], sems.at[s]))
        copies[-1].start()
    for copy in copies:
        copy.wait()


def swap(values, partner, wide_size, narrow_size):
    pairs = []
    for w in range(wide_size):
        for n in range(narrow_size):
            wide, narrow = partner(w, n)
            pairs.append((w * narrow_size + n, wide * narrow_size + narrow))
    return lax.ppermute(values, BOTH, pairs)


def bits(first, last):
    while first < last:
        yield first
        first *= 2


def max_over_chips(values, wide_size, narrow_size):
    steps = [(bit, 1) for bit in bits(1, wide_size)]
    steps += [(0, bit + 1) for bit in bits(2, narrow_size)]
    for wide_bit, narrow_bit in steps:
        other = swap(
            values, lambda w, n: (w ^ wide_bit, n ^ narrow_bit), wide_size, narrow_size
        )
        values = jnp.maximum(values, other)
    return values


def window_max(values, start, window):
    old = lax.dynamic_slice_in_dim(values, start, window.shape[0], 0)
    return lax.dynamic_update_slice_in_dim(values, jnp.maximum(old, window), start, 0)


def swap_in_chip(values, places, wide_size, narrow_size):
    columns = values.shape[0] // narrow_size
    row_start = lax.axis_index("wide") * ROWB
    n = lax.axis_index("narrow")
    sent = jnp.concatenate(
        [
            lax.dynamic_slice_in_dim(values, n * columns, columns, 0),
            lax.dynamic_slice_in_dim(values, row_start, ROWB, 0),
            places,
        ]
    )
    other = swap(sent, lambda w, n: (w, n ^ 1), wide_size, narrow_size)
    values = window_max(values, (n ^ 1) * columns, other[:columns])
    return window_max(values, row_start, other[columns:-1]), other[-1:]


def windows(values, wide_size, narrow_size):
    size = 2 * values.shape[0] // narrow_size
    columns = (lax.axis_index("narrow") >> 1) * size
    rows = lax.axis_index("wide") // (2 * wide_size // narrow_size) * size
    return columns, rows, size


def max_over_users(values, wide_size, narrow_size):
    share = wide_size // narrow_size

    def along_columns(w, n):
        lane = n ^ n >> 1
        for bit in bits(1, wide_size):
            lane = lane ^ w // bit
        return lane & 1 == 0

    def first(w, n):
        return (w ^ share, n ^ 1) if along_columns(w, n) else (w, n ^ 3)

    def second(w, n):
        return (w ^ 2 * share if along_columns(w, n) else w ^ share, n ^ 1)

    columns, rows, size = windows(values, wide_size, narrow_size)
    chosen = along_columns(lax.axis_index("wide"), lax.axis_index("narrow"))
    start = jnp.where(chosen, columns, rows)
    window = lax.dynamic_slice_in_dim(values, start, size, 0)
    for bit in bits(1, share):
        other = swap(window, lambda w, n: (w ^ bit, n ^ 1), wide_size, narrow_size)
        window = jnp.maximum(window, other)
    for partner in (first, second):
        window = jnp.maximum(window, swap(window, partner, wide_size, narrow_size))
    other = swap(window, lambda w, n: (w, n ^ 1), wide_size, narrow_size)
    values = window_max(values, start, window)
    return window_max(values, jnp.where(chosen, rows, columns), other)


def max_of_rows_too(values, wide_size, narrow_size):
    columns, rows, size = windows(values, wide_size, narrow_size)
    share, group_size = wide_size // narrow_size, size // 2
    w, n = lax.axis_index("wide"), lax.axis_index("narrow")
    group = w // share
    for bit in bits(1, wide_size // 2):
        group_start = (group if bit < share else group | 1) * group_size
        sent = jnp.concatenate(
            [
                lax.dynamic_slice_in_dim(values, columns, size, 0),
                lax.dynamic_slice_in_dim(values, group_start, group_size, 0),
            ]
        )
        other = swap(sent, lambda w, n: (w ^ bit, n ^ 1), wide_size, narrow_size)
        values = window_max(values, columns, other[:size])
        values = window_max(values, group_start, other[size:])
    half = wide_size // 2
    by_columns = swap(
        lax.dynamic_slice_in_dim(values, columns, size, 0),
        lambda w, n: (w ^ half if n > 1 else w, n ^ 1),
        wide_size,
        narrow_size,
    )
    by_rows = swap(
        lax.dynamic_slice_in_dim(values, rows, size, 0),
        lambda w, n: (w, n ^ 3 if w < half else n ^ 1),
        wide_size,
        narrow_size,
    )
    by_columns, by_rows = lax.optimization_barrier((by_columns, by_rows))
    values = window_max(values, columns, by_columns)
    row_start = w * ROWB
    given = swap(
        lax.dynamic_slice_in_dim(values, row_start, ROWB, 0),
        lambda w, n: (w, n ^ 1 if w < half else n ^ 3),
        wide_size,
        narrow_size,
    )
    values = window_max(values, rows, by_rows)
    own = lax.dynamic_slice_in_dim(values, row_start, ROWB, 0)
    return values, jnp.where((w >= half) & (n < 2), given, own)


def on_device(wide_size, narrow_size, tiles, tile_rows, tile_cols, tile_counts):
    slots, tile = tiles.shape[1], tiles.shape[2]
    blocks = ROWB * wide_size
    four = narrow_size == 4
    sizes = [min(PIECE, slots - s) for s in range(0, slots, PIECE)]
    rows, cols, part, index, *held = pl.pallas_call(
        first_kernel,
        out_shape=(
            pltpu.SMEM(tile_rows.shape, jnp.int32),
            pltpu.SMEM(tile_cols.shape, jnp.int32),
            pltpu.VMEM((blocks, tile), jnp.float32),
            pltpu.VMEM((1, tile), jnp.float32),
            *[pltpu.VMEM((size, tile, tile), jnp.float32) for size in sizes],
        ),
        in_specs=[SMEM, HBM, HBM, HBM],
        out_specs=(SMEM, SMEM, VMEM, VMEM, *[VMEM for size in sizes]),
        scratch_shapes=[pltpu.SemaphoreType.DMA((2 + slots,))],
        compiler_params=PARAMS,
        name="first_peaks",
    )(tile_counts, *kept((tile_rows, tile_cols, tiles), pltpu.HBM))
    places = (*kept((rows, cols), pltpu.SMEM), tile_counts)
    part, index = swap_in_chip(part, index, wide_size, narrow_size)
    part, *sent = lax.optimization_barrier((part, *held))
    mates = [swap(piece, lambda w, n: (w, n ^ 1), wide_size, narrow_size) for piece in sent]
    held = kept(held, pltpu.VMEM)
    mate_places = pl.pallas_call(
        places_kernel,
        out_shape=pltpu.SMEM(index.shape, jnp.int32),
        in_specs=[VMEM],
        out_specs=SMEM,
        scratch_shapes=[pltpu.VMEM(index.shape, jnp.int32), pltpu.SemaphoreType.DMA((1,))],
        compiler_params=PARAMS,
        name="other_places",
    )(*kept([index], pltpu.VMEM))
    places_too = (*places, *kept([mate_places], pltpu.SMEM))
    for iteration in range(1, ITERS):
        full = (max_over_users if four else max_over_chips)(part, wide_size, narrow_size)
        part = pl.pallas_call(
            functools.partial(next_kernel, ROWB),
            out_shape=pltpu.VMEM((blocks, tile), jnp.float32),
            in_specs=[SMEM] * 4 + [VMEM] * (1 + 2 * len(held)),
            out_specs=VMEM,
            scratch_shapes=[
                pltpu.VMEM((blocks, tile), jnp.float32),
                pltpu.VMEM((ROWB, tile, tile // 2), jnp.float32),
            ],
            compiler_params=PARAMS,
            name="next_peaks",
        )(*places_too, *kept([full], pltpu.VMEM), *held, *kept(mates, pltpu.VMEM))
    if four:
        full, own = max_of_rows_too(part, wide_size, narrow_size)
    else:
        full = max_over_chips(part, wide_size, narrow_size)
        own = lax.dynamic_slice_in_dim(full, lax.axis_index("wide") * ROWB, ROWB, 0)
    result = pl.pallas_call(
        last_kernel,
        out_shape=jax.ShapeDtypeStruct(tiles.shape, jnp.float32),
        in_specs=[SMEM] * 3 + [VMEM] * (1 + len(held)),
        out_specs=HBM,
        scratch_shapes=[
            pltpu.VMEM((blocks, tile), jnp.float32),
            pltpu.VMEM((slots, tile, tile), jnp.float32),
            pltpu.SemaphoreType.DMA((slots,)),
        ],
        cost_estimate=pl.CostEstimate(
            flops=2 * tiles.size, bytes_accessed=8 * tiles.size, transcendentals=0
        ),
        compiler_params=PARAMS,
        name="scaled_tiles",
    )(*places, *kept([full], pltpu.VMEM), *held)
    return result, lax.rsqrt(own)


def solution(mesh):
    wide_size, narrow_size = mesh.shape["wide"], mesh.shape["narrow"]
    placed = (
        P("wide", "narrow", None, None),
        P("wide", "narrow"),
        P("wide", "narrow"),
        P("wide", "narrow"),
    )
    return jax.shard_map(
        functools.partial(on_device, wide_size, narrow_size),
        mesh=mesh,
        in_specs=placed,
        out_specs=(P("wide", "narrow", None, None), P("wide", None)),
        check_vma=False,
    )
```

```python
import functools

import jax
import jax.numpy as jnp
from jax import lax
from jax.experimental import pallas as pl
from jax.experimental.pallas import tpu as pltpu
from jax.sharding import PartitionSpec as P

ROWB = 4
ITERS = 2
PIECE = 2
PARAMS = pltpu.CompilerParams(vmem_limit_bytes=16 << 20)
BOTH = ("wide", "narrow")
SMEM = pl.BlockSpec(memory_space=pltpu.SMEM)
VMEM = pl.BlockSpec(memory_space=pltpu.VMEM)
HBM = pl.BlockSpec(memory_space=pltpu.HBM)


def kept(values, space):
    return [pltpu.with_memory_space_constraint(value, space) for value in values]


def raise_row(peak_ref, index, row):
    peak_ref[pl.ds(index, 1), :] = jnp.maximum(peak_ref[pl.ds(index, 1), :], row)


def lane_max(block):
    half = block.shape[1] // 2
    folded = jnp.maximum(block[:, :half], block[:, half:])
    return jnp.max(folded.T, axis=0, keepdims=True)


def as_column(row, half):
    return jnp.broadcast_to(row, (half, row.shape[1])).T


def first_kernel(
    count_ref,
    rows_in,
    cols_in,
    tiles_ref,
    rows_ref,
    cols_ref,
    peak_ref,
    places_ref,
    *refs,
):
    *held_refs, sems = refs
    slots = tiles_ref.shape[1]
    held = [ref.at[s] for ref in held_refs for s in range(ref.shape[0])]
    moves = [(rows_in, rows_ref), (cols_in, cols_ref)]
    moves += [(tiles_ref.at[0, s], held[s]) for s in range(slots)]
    copies = [
        pltpu.make_async_copy(source, target, sems.at[k])
        for k, (source, target) in enumerate(moves)
    ]
    for copy in copies:
        copy.start()
    peak_ref[...] = jnp.zeros_like(peak_ref)
    for copy in copies[:2]:
        copy.wait()
    values = [count_ref[0, 0]]
    values += [ref[0, s] for s in range(slots) for ref in (rows_ref, cols_ref)]
    lane = lax.broadcasted_iota(jnp.int32, places_ref.shape, 1)
    places = jnp.zeros(places_ref.shape, jnp.int32)
    for k, value in enumerate(values):
        places = jnp.where(lane == k, value, places)
    places_ref[...] = places.astype(jnp.float32)
    for first in range(0, slots, 2):
        found = []
        for copy in copies[2 + first : 4 + first]:
            copy.wait()
        for s in range(first, min(first + 2, slots)):
            size = jnp.abs(held[s][...])
            found.append((s, jnp.max(size, axis=0, keepdims=True), lane_max(size)))
        for s, column_max, row_max in found:
            live = s < count_ref[0, 0]
            raise_row(peak_ref, cols_ref[0, s], jnp.where(live, column_max, 0.0))
            raise_row(peak_ref, rows_ref[0, s], jnp.where(live, row_max, 0.0))


def places_kernel(index_ref, places_ref, whole_ref, sem):
    whole_ref[...] = index_ref[...].astype(jnp.int32)
    copy = pltpu.make_async_copy(whole_ref, places_ref, sem.at[0])
    copy.start()
    copy.wait()


def next_kernel(row_blocks, rows_ref, cols_ref, count_ref, mate_places, old_ref, *refs):
    *tile_refs, peak_ref, scale_ref, column_ref = refs
    tiles = [ref.at[s] for ref in tile_refs for s in range(ref.shape[0])]
    slots, tile = len(tiles) // 2, tiles[0].shape[0]
    half = tile // 2
    scale_ref[...] = lax.rsqrt(old_ref[...])
    peak_ref[...] = jnp.zeros_like(peak_ref)
    start = lax.axis_index("wide") * row_blocks
    for k in range(row_blocks):
        column_ref[k] = as_column(scale_ref[pl.ds(start + k, 1), :], half)

    def add(tiles, count, places):
        found = []
        for tile_ref, (row, col) in zip(tiles, places):
            size = jnp.abs(tile_ref[...])
            left = scale_ref[pl.ds(row, 1), :]
            right = scale_ref[pl.ds(col, 1), :]
            row_max = lane_max(size * right) * left
            column = column_ref[row - start]
            below = jnp.concatenate(
                [
                    jnp.max(size[:, :half] * column, axis=0, keepdims=True),
                    jnp.max(size[:, half:] * column, axis=0, keepdims=True),
                ],
                axis=1,
            )
            found.append((row_max, below * right))
        for s, (row_max, column_max) in enumerate(found):
            raise_row(peak_ref, places[s][0], jnp.where(s < count, row_max, 0.0))
            raise_row(peak_ref, places[s][1], jnp.where(s < count, column_max, 0.0))

    given = [mate_places[0, k] for k in range(2 * slots + 1)]
    own = [(rows_ref[0, s], cols_ref[0, s]) for s in range(slots)]
    add(tiles[:slots], count_ref[0, 0], own)
    add(tiles[slots:], given[0], list(zip(given[1::2], given[2::2])))
    peak_ref[...] = peak_ref[...] * old_ref[...]


def last_kernel(row_blocks, rows_ref, cols_ref, count_ref, old_ref, *refs):
    *held_refs, out_ref, own_out, scale_ref, own_ref, done_ref, sems = refs
    held = [ref.at[s] for ref in held_refs for s in range(ref.shape[0])]
    slots, tile = len(held), held[0].shape[0]
    half = tile // 2
    scale_ref[...] = lax.rsqrt(old_ref[...])
    start = lax.axis_index("wide") * row_blocks
    for k in range(row_blocks):
        own_ref[pl.ds(k, 1), :] = scale_ref[pl.ds(start + k, 1), :]
    copies = [pltpu.make_async_copy(own_ref, own_out, sems.at[slots])]
    copies[0].start()
    for s in range(slots):
        live = s < count_ref[0, 0]
        left = scale_ref[pl.ds(rows_ref[0, s], 1), :]
        right = scale_ref[pl.ds(cols_ref[0, s], 1), :]
        column = as_column(left, half)
        for part in (slice(0, half), slice(half, tile)):
            scaled = held[s][:, part] * column * right[:, part]
            done_ref[s, :, part] = jnp.where(live, scaled, 0.0)
        copies.append(pltpu.make_async_copy(done_ref.at[s], out_ref.at[0, s], sems.at[s]))
        copies[-1].start()
    for copy in copies:
        copy.wait()


def given_kernel(half, given_ref, own_ref, out_ref, scale_ref, sem):
    del own_ref
    w, n = lax.axis_index("wide"), lax.axis_index("narrow")

    @pl.when((w >= half) & (n < 2))
    def _():
        scale_ref[...] = lax.rsqrt(given_ref[...])
        copy = pltpu.make_async_copy(scale_ref, out_ref, sem.at[0])
        copy.start()
        copy.wait()


def swap(values, partner, wide_size, narrow_size):
    pairs = []
    for w in range(wide_size):
        for n in range(narrow_size):
            wide, narrow = partner(w, n)
            pairs.append((w * narrow_size + n, wide * narrow_size + narrow))
    return lax.ppermute(values, BOTH, pairs)


def bits(first, last):
    while first < last:
        yield first
        first *= 2


def max_over_chips(values, wide_size, narrow_size):
    steps = [(bit, 1) for bit in bits(1, wide_size)]
    steps += [(0, bit + 1) for bit in bits(2, narrow_size)]
    for wide_bit, narrow_bit in steps:
        other = swap(
            values, lambda w, n: (w ^ wide_bit, n ^ narrow_bit), wide_size, narrow_size
        )
        values = jnp.maximum(values, other)
    return values


def window_max(values, start, window):
    old = lax.dynamic_slice_in_dim(values, start, window.shape[0], 0)
    return lax.dynamic_update_slice_in_dim(values, jnp.maximum(old, window), start, 0)


def swap_in_chip(values, places, wide_size, narrow_size):
    columns = values.shape[0] // narrow_size
    row_start = lax.axis_index("wide") * ROWB
    n = lax.axis_index("narrow")
    sent = jnp.concatenate(
        [
            lax.dynamic_slice_in_dim(values, n * columns, columns, 0),
            lax.dynamic_slice_in_dim(values, row_start, ROWB, 0),
            places,
        ]
    )
    other = swap(sent, lambda w, n: (w, n ^ 1), wide_size, narrow_size)
    values = window_max(values, (n ^ 1) * columns, other[:columns])
    return window_max(values, row_start, other[columns:-1]), other[-1:]


def windows(values, wide_size, narrow_size):
    size = 2 * values.shape[0] // narrow_size
    columns = (lax.axis_index("narrow") >> 1) * size
    rows = lax.axis_index("wide") // (2 * wide_size // narrow_size) * size
    return columns, rows, size


def max_over_users(values, wide_size, narrow_size):
    columns, rows, size = windows(values, wide_size, narrow_size)
    share, group_size = wide_size // narrow_size, size // 2
    half = wide_size // 2
    w, n = lax.axis_index("wide"), lax.axis_index("narrow")
    group = w // share
    for bit in bits(1, half):
        group_start = (group if bit < share else group | 1) * group_size
        sent = jnp.concatenate(
            [
                lax.dynamic_slice_in_dim(values, columns, size, 0),
                lax.dynamic_slice_in_dim(values, group_start, group_size, 0),
            ]
        )
        other = swap(sent, lambda w, n: (w ^ bit, n ^ 1), wide_size, narrow_size)
        values = window_max(values, columns, other[:size])
        values = window_max(values, group_start, other[size:])
    by_columns = swap(
        lax.dynamic_slice_in_dim(values, columns, size, 0),
        lambda w, n: (w ^ half if n > 1 else w, n ^ 1),
        wide_size,
        narrow_size,
    )
    by_rows = swap(
        lax.dynamic_slice_in_dim(values, rows, size, 0),
        lambda w, n: (w, n ^ 3 if w < half else n ^ 1),
        wide_size,
        narrow_size,
    )
    by_columns, by_rows = lax.optimization_barrier((by_columns, by_rows))
    merged = window_max(values, columns, by_columns)

    def rows_too():
        own = lax.dynamic_slice_in_dim(merged, w * ROWB, ROWB, 0)
        return swap(
            own, lambda w, n: (w, n ^ 1 if w < half else n ^ 3), wide_size, narrow_size
        )

    return window_max(merged, rows, by_rows), rows_too


def on_device(wide_size, narrow_size, tiles, tile_rows, tile_cols, tile_counts):
    slots, tile = tiles.shape[1], tiles.shape[2]
    blocks = ROWB * wide_size
    four = narrow_size == 4
    sizes = [min(PIECE, slots - s) for s in range(0, slots, PIECE)]
    rows, cols, part, index, *held = pl.pallas_call(
        first_kernel,
        out_shape=(
            pltpu.SMEM(tile_rows.shape, jnp.int32),
            pltpu.SMEM(tile_cols.shape, jnp.int32),
            pltpu.VMEM((blocks, tile), jnp.float32),
            pltpu.VMEM((1, tile), jnp.float32),
            *[pltpu.VMEM((size, tile, tile), jnp.float32) for size in sizes],
        ),
        in_specs=[SMEM, HBM, HBM, HBM],
        out_specs=(SMEM, SMEM, VMEM, VMEM, *[VMEM for size in sizes]),
        scratch_shapes=[pltpu.SemaphoreType.DMA((2 + slots,))],
        compiler_params=PARAMS,
        name="first_peaks",
    )(tile_counts, *kept((tile_rows, tile_cols, tiles), pltpu.HBM))
    places = (*kept((rows, cols), pltpu.SMEM), tile_counts)
    part, index = swap_in_chip(part, index, wide_size, narrow_size)
    part, *sent = lax.optimization_barrier((part, *held))
    mates = [swap(piece, lambda w, n: (w, n ^ 1), wide_size, narrow_size) for piece in sent]
    held = kept(held, pltpu.VMEM)
    mate_places = pl.pallas_call(
        places_kernel,
        out_shape=pltpu.SMEM(index.shape, jnp.int32),
        in_specs=[VMEM],
        out_specs=SMEM,
        scratch_shapes=[pltpu.VMEM(index.shape, jnp.int32), pltpu.SemaphoreType.DMA((1,))],
        compiler_params=PARAMS,
        name="other_places",
    )(*kept([index], pltpu.VMEM))
    places_too = (*places, *kept([mate_places], pltpu.SMEM))
    for iteration in range(1, ITERS):
        if four:
            full, _ = max_over_users(part, wide_size, narrow_size)
        else:
            full = max_over_chips(part, wide_size, narrow_size)
        part = pl.pallas_call(
            functools.partial(next_kernel, ROWB),
            out_shape=pltpu.VMEM((blocks, tile), jnp.float32),
            in_specs=[SMEM] * 4 + [VMEM] * (1 + 2 * len(held)),
            out_specs=VMEM,
            scratch_shapes=[
                pltpu.VMEM((blocks, tile), jnp.float32),
                pltpu.VMEM((ROWB, tile, tile // 2), jnp.float32),
            ],
            compiler_params=PARAMS,
            name="next_peaks",
        )(*places_too, *kept([full], pltpu.VMEM), *held, *kept(mates, pltpu.VMEM))
    if four:
        full, rows_too = max_over_users(part, wide_size, narrow_size)
    else:
        full = max_over_chips(part, wide_size, narrow_size)
    own_shape = jax.ShapeDtypeStruct((ROWB, tile), jnp.float32)
    result, own = pl.pallas_call(
        functools.partial(last_kernel, ROWB),
        out_shape=(jax.ShapeDtypeStruct(tiles.shape, jnp.float32), own_shape),
        in_specs=[SMEM] * 3 + [VMEM] * (1 + len(held)),
        out_specs=(HBM, HBM),
        scratch_shapes=[
            pltpu.VMEM((blocks, tile), jnp.float32),
            pltpu.VMEM((ROWB, tile), jnp.float32),
            pltpu.VMEM((slots, tile, tile), jnp.float32),
            pltpu.SemaphoreType.DMA((slots + 1,)),
        ],
        cost_estimate=pl.CostEstimate(
            flops=2 * tiles.size, bytes_accessed=8 * tiles.size, transcendentals=0
        ),
        compiler_params=PARAMS,
        name="scaled_tiles",
    )(*places, *kept([full], pltpu.VMEM), *held)
    if four:
        own = pl.pallas_call(
            functools.partial(given_kernel, wide_size // 2),
            out_shape=own_shape,
            in_specs=[VMEM, HBM],
            out_specs=HBM,
            scratch_shapes=[
                pltpu.VMEM((ROWB, tile), jnp.float32),
                pltpu.SemaphoreType.DMA((1,)),
            ],
            input_output_aliases={1: 0},
            compiler_params=PARAMS,
            name="given_scaling",
        )(*kept([rows_too()], pltpu.VMEM), own)
    return result, own


def solution(mesh):
    wide_size, narrow_size = mesh.shape["wide"], mesh.shape["narrow"]
    placed = (
        P("wide", "narrow", None, None),
        P("wide", "narrow"),
        P("wide", "narrow"),
        P("wide", "narrow"),
    )
    return jax.shard_map(
        functools.partial(on_device, wide_size, narrow_size),
        mesh=mesh,
        in_specs=placed,
        out_specs=(P("wide", "narrow", None, None), P("wide", None)),
        check_vma=False,
    )
```

```python
import functools

import jax
import jax.numpy as jnp
from jax import lax
from jax.experimental import pallas as pl
from jax.experimental.pallas import tpu as pltpu
from jax.sharding import PartitionSpec as P

ROWB = 4
ITERS = 2
PIECE = 2
PARAMS = pltpu.CompilerParams(vmem_limit_bytes=16 << 20)
BOTH = ("wide", "narrow")
SMEM = pl.BlockSpec(memory_space=pltpu.SMEM)
VMEM = pl.BlockSpec(memory_space=pltpu.VMEM)
HBM = pl.BlockSpec(memory_space=pltpu.HBM)


def kept(values, space):
    return [pltpu.with_memory_space_constraint(value, space) for value in values]


def raise_row(peak_ref, index, row):
    peak_ref[pl.ds(index, 1), :] = jnp.maximum(peak_ref[pl.ds(index, 1), :], row)


def lane_max(block):
    half = block.shape[1] // 2
    folded = jnp.maximum(block[:, :half], block[:, half:])
    return jnp.max(folded.T, axis=0, keepdims=True)


def as_column(row, half):
    return jnp.broadcast_to(row, (half, row.shape[1])).T


def first_kernel(
    count_ref,
    rows_in,
    cols_in,
    tiles_ref,
    rows_ref,
    cols_ref,
    peak_ref,
    places_ref,
    *refs,
):
    *held_refs, sems = refs
    slots = tiles_ref.shape[1]
    held = [ref.at[s] for ref in held_refs for s in range(ref.shape[0])]
    moves = [(rows_in, rows_ref), (cols_in, cols_ref)]
    moves += [(tiles_ref.at[0, s], held[s]) for s in range(slots)]
    copies = [
        pltpu.make_async_copy(source, target, sems.at[k])
        for k, (source, target) in enumerate(moves)
    ]
    for copy in copies:
        copy.start()
    peak_ref[...] = jnp.zeros_like(peak_ref)
    for copy in copies[:2]:
        copy.wait()
    values = [count_ref[0, 0]]
    values += [ref[0, s] for s in range(slots) for ref in (rows_ref, cols_ref)]
    lane = lax.broadcasted_iota(jnp.int32, places_ref.shape, 1)
    places = jnp.zeros(places_ref.shape, jnp.int32)
    for k, value in enumerate(values):
        places = jnp.where(lane == k, value, places)
    places_ref[...] = places.astype(jnp.float32)
    for first in range(0, slots, 2):
        found = []
        for copy in copies[2 + first : 4 + first]:
            copy.wait()
        for s in range(first, min(first + 2, slots)):
            size = jnp.abs(held[s][...])
            found.append((s, jnp.max(size, axis=0, keepdims=True), lane_max(size)))
        for s, column_max, row_max in found:
            live = s < count_ref[0, 0]
            raise_row(peak_ref, cols_ref[0, s], jnp.where(live, column_max, 0.0))
            raise_row(peak_ref, rows_ref[0, s], jnp.where(live, row_max, 0.0))


def places_kernel(index_ref, places_ref, whole_ref, sem):
    whole_ref[...] = index_ref[...].astype(jnp.int32)
    copy = pltpu.make_async_copy(whole_ref, places_ref, sem.at[0])
    copy.start()
    copy.wait()


def next_kernel(row_blocks, rows_ref, cols_ref, count_ref, mate_places, old_ref, *refs):
    *tile_refs, peak_ref, scale_ref, column_ref = refs
    tiles = [ref.at[s] for ref in tile_refs for s in range(ref.shape[0])]
    slots, tile = len(tiles) // 2, tiles[0].shape[0]
    half = tile // 2
    scale_ref[...] = lax.rsqrt(old_ref[...])
    peak_ref[...] = jnp.zeros_like(peak_ref)
    start = lax.axis_index("wide") * row_blocks
    for k in range(row_blocks):
        column_ref[k] = as_column(scale_ref[pl.ds(start + k, 1), :], half)

    def add(tiles, count, places):
        found = []
        for tile_ref, (row, col) in zip(tiles, places):
            size = jnp.abs(tile_ref[...])
            left = scale_ref[pl.ds(row, 1), :]
            right = scale_ref[pl.ds(col, 1), :]
            row_max = lane_max(size * right) * left
            column = column_ref[row - start]
            below = jnp.concatenate(
                [
                    jnp.max(size[:, :half] * column, axis=0, keepdims=True),
                    jnp.max(size[:, half:] * column, axis=0, keepdims=True),
                ],
                axis=1,
            )
            found.append((row_max, below * right))
        for s, (row_max, column_max) in enumerate(found):
            raise_row(peak_ref, places[s][0], jnp.where(s < count, row_max, 0.0))
            raise_row(peak_ref, places[s][1], jnp.where(s < count, column_max, 0.0))

    given = [mate_places[0, k] for k in range(2 * slots + 1)]
    own = [(rows_ref[0, s], cols_ref[0, s]) for s in range(slots)]
    add(tiles[:slots], count_ref[0, 0], own)
    add(tiles[slots:], given[0], list(zip(given[1::2], given[2::2])))
    peak_ref[...] = peak_ref[...] * old_ref[...]


def last_kernel(row_blocks, rows_ref, cols_ref, count_ref, old_ref, *refs):
    *held_refs, out_ref, own_out, scale_ref, own_ref, done_ref, sems = refs
    held = [ref.at[s] for ref in held_refs for s in range(ref.shape[0])]
    slots, tile = len(held), held[0].shape[0]
    half = tile // 2
    scale_ref[...] = lax.rsqrt(old_ref[...])
    start = lax.axis_index("wide") * row_blocks
    for k in range(row_blocks):
        own_ref[pl.ds(k, 1), :] = scale_ref[pl.ds(start + k, 1), :]
    copies = [pltpu.make_async_copy(own_ref, own_out, sems.at[slots])]
    copies[0].start()
    for s in range(slots):
        live = s < count_ref[0, 0]
        left = scale_ref[pl.ds(rows_ref[0, s], 1), :]
        right = scale_ref[pl.ds(cols_ref[0, s], 1), :]
        column = as_column(left, half)
        for part in (slice(0, half), slice(half, tile)):
            scaled = held[s][:, part] * column * right[:, part]
            done_ref[s, :, part] = jnp.where(live, scaled, 0.0)
        copies.append(pltpu.make_async_copy(done_ref.at[s], out_ref.at[0, s], sems.at[s]))
        copies[-1].start()
    for copy in copies:
        copy.wait()


def given_kernel(half, given_ref, own_ref, out_ref, scale_ref, sem):
    del own_ref
    w, n = lax.axis_index("wide"), lax.axis_index("narrow")

    @pl.when((w >= half) & (n < 2))
    def _():
        scale_ref[...] = lax.rsqrt(given_ref[...])
        copy = pltpu.make_async_copy(scale_ref, out_ref, sem.at[0])
        copy.start()
        copy.wait()


def swap(values, partner, wide_size, narrow_size):
    pairs = []
    for w in range(wide_size):
        for n in range(narrow_size):
            wide, narrow = partner(w, n)
            pairs.append((w * narrow_size + n, wide * narrow_size + narrow))
    return lax.ppermute(values, BOTH, pairs)


def bits(first, last):
    while first < last:
        yield first
        first *= 2


def max_over_chips(values, wide_size, narrow_size):
    steps = [(bit, 1) for bit in bits(1, wide_size)]
    steps += [(0, bit + 1) for bit in bits(2, narrow_size)]
    for wide_bit, narrow_bit in steps:
        other = swap(
            values, lambda w, n: (w ^ wide_bit, n ^ narrow_bit), wide_size, narrow_size
        )
        values = jnp.maximum(values, other)
    return values


def window_max(values, start, window):
    old = lax.dynamic_slice_in_dim(values, start, window.shape[0], 0)
    return lax.dynamic_update_slice_in_dim(values, jnp.maximum(old, window), start, 0)


def swap_in_chip(values, places, wide_size, narrow_size):
    columns = values.shape[0] // narrow_size
    row_start = lax.axis_index("wide") * ROWB
    n = lax.axis_index("narrow")
    sent = jnp.concatenate(
        [
            lax.dynamic_slice_in_dim(values, n * columns, columns, 0),
            lax.dynamic_slice_in_dim(values, row_start, ROWB, 0),
            places,
        ]
    )
    other = swap(sent, lambda w, n: (w, n ^ 1), wide_size, narrow_size)
    values = window_max(values, (n ^ 1) * columns, other[:columns])
    return window_max(values, row_start, other[columns:-1]), other[-1:]


def windows(values, wide_size, narrow_size):
    size = 2 * values.shape[0] // narrow_size
    columns = (lax.axis_index("narrow") >> 1) * size
    rows = lax.axis_index("wide") // (2 * wide_size // narrow_size) * size
    return columns, rows, size


def max_over_users(values, wide_size, narrow_size, idle):
    columns, rows, size = windows(values, wide_size, narrow_size)
    share, group_size = wide_size // narrow_size, size // 2
    half = wide_size // 2
    w, n = lax.axis_index("wide"), lax.axis_index("narrow")
    group = w // share
    for bit in bits(1, half):
        group_start = (group if bit < share else group | 1) * group_size
        sent = jnp.concatenate(
            [
                lax.dynamic_slice_in_dim(values, columns, size, 0),
                lax.dynamic_slice_in_dim(values, group_start, group_size, 0),
            ]
        )
        other = swap(sent, lambda w, n: (w ^ bit, n ^ 1), wide_size, narrow_size)
        values = window_max(values, columns, other[:size])
        values = window_max(values, group_start, other[size:])
    by_columns = swap(
        lax.dynamic_slice_in_dim(values, columns, size, 0),
        lambda w, n: (w ^ half if n > 1 else w, n ^ 1),
        wide_size,
        narrow_size,
    )
    by_rows = swap(
        lax.dynamic_slice_in_dim(values, rows, size, 0),
        lambda w, n: (w, n ^ (3 if w < half else idle)),
        wide_size,
        narrow_size,
    )
    by_columns, by_rows = lax.optimization_barrier((by_columns, by_rows))
    merged = window_max(values, columns, by_columns)

    def rows_too():
        own = lax.dynamic_slice_in_dim(merged, w * ROWB, ROWB, 0)
        return swap(
            own, lambda w, n: (w, n ^ 1 if w < half else n ^ 3), wide_size, narrow_size
        )

    return window_max(merged, rows, by_rows), rows_too


def on_device(wide_size, narrow_size, tiles, tile_rows, tile_cols, tile_counts):
    slots, tile = tiles.shape[1], tiles.shape[2]
    blocks = ROWB * wide_size
    four = narrow_size == 4
    sizes = [min(PIECE, slots - s) for s in range(0, slots, PIECE)]
    rows, cols, part, index, *held = pl.pallas_call(
        first_kernel,
        out_shape=(
            pltpu.SMEM(tile_rows.shape, jnp.int32),
            pltpu.SMEM(tile_cols.shape, jnp.int32),
            pltpu.VMEM((blocks, tile), jnp.float32),
            pltpu.VMEM((1, tile), jnp.float32),
            *[pltpu.VMEM((size, tile, tile), jnp.float32) for size in sizes],
        ),
        in_specs=[SMEM, HBM, HBM, HBM],
        out_specs=(SMEM, SMEM, VMEM, VMEM, *[VMEM for size in sizes]),
        scratch_shapes=[pltpu.SemaphoreType.DMA((2 + slots,))],
        compiler_params=PARAMS,
        name="first_peaks",
    )(tile_counts, *kept((tile_rows, tile_cols, tiles), pltpu.HBM))
    places = (*kept((rows, cols), pltpu.SMEM), tile_counts)
    part, index = swap_in_chip(part, index, wide_size, narrow_size)
    part, *sent = lax.optimization_barrier((part, *held))
    mates = [swap(piece, lambda w, n: (w, n ^ 1), wide_size, narrow_size) for piece in sent]
    held = kept(held, pltpu.VMEM)
    mate_places = pl.pallas_call(
        places_kernel,
        out_shape=pltpu.SMEM(index.shape, jnp.int32),
        in_specs=[VMEM],
        out_specs=SMEM,
        scratch_shapes=[pltpu.VMEM(index.shape, jnp.int32), pltpu.SemaphoreType.DMA((1,))],
        compiler_params=PARAMS,
        name="other_places",
    )(*kept([index], pltpu.VMEM))
    places_too = (*places, *kept([mate_places], pltpu.SMEM))
    for iteration in range(1, ITERS):
        if four:
            full, _ = max_over_users(part, wide_size, narrow_size, 1)
        else:
            full = max_over_chips(part, wide_size, narrow_size)
        part = pl.pallas_call(
            functools.partial(next_kernel, ROWB),
            out_shape=pltpu.VMEM((blocks, tile), jnp.float32),
            in_specs=[SMEM] * 4 + [VMEM] * (1 + 2 * len(held)),
            out_specs=VMEM,
            scratch_shapes=[
                pltpu.VMEM((blocks, tile), jnp.float32),
                pltpu.VMEM((ROWB, tile, tile // 2), jnp.float32),
            ],
            compiler_params=PARAMS,
            name="next_peaks",
        )(*places_too, *kept([full], pltpu.VMEM), *held, *kept(mates, pltpu.VMEM))
    if four:
        full, rows_too = max_over_users(part, wide_size, narrow_size, 3)
    else:
        full = max_over_chips(part, wide_size, narrow_size)
    own_shape = jax.ShapeDtypeStruct((ROWB, tile), jnp.float32)
    result, own = pl.pallas_call(
        functools.partial(last_kernel, ROWB),
        out_shape=(jax.ShapeDtypeStruct(tiles.shape, jnp.float32), own_shape),
        in_specs=[SMEM] * 3 + [VMEM] * (1 + len(held)),
        out_specs=(HBM, HBM),
        scratch_shapes=[
            pltpu.VMEM((blocks, tile), jnp.float32),
            pltpu.VMEM((ROWB, tile), jnp.float32),
            pltpu.VMEM((slots, tile, tile), jnp.float32),
            pltpu.SemaphoreType.DMA((slots + 1,)),
        ],
        cost_estimate=pl.CostEstimate(
            flops=2 * tiles.size, bytes_accessed=8 * tiles.size, transcendentals=0
        ),
        compiler_params=PARAMS,
        name="scaled_tiles",
    )(*places, *kept([full], pltpu.VMEM), *held)
    if four:
        own = pl.pallas_call(
            functools.partial(given_kernel, wide_size // 2),
            out_shape=own_shape,
            in_specs=[VMEM, HBM],
            out_specs=HBM,
            scratch_shapes=[
                pltpu.VMEM((ROWB, tile), jnp.float32),
                pltpu.SemaphoreType.DMA((1,)),
            ],
            input_output_aliases={1: 0},
            compiler_params=PARAMS,
            name="given_scaling",
        )(*kept([rows_too()], pltpu.VMEM), own)
    return result, own


def solution(mesh):
    wide_size, narrow_size = mesh.shape["wide"], mesh.shape["narrow"]
    placed = (
        P("wide", "narrow", None, None),
        P("wide", "narrow"),
        P("wide", "narrow"),
        P("wide", "narrow"),
    )
    return jax.shard_map(
        functools.partial(on_device, wide_size, narrow_size),
        mesh=mesh,
        in_specs=placed,
        out_specs=(P("wide", "narrow", None, None), P("wide", None)),
        check_vma=False,
    )
```

```python
import functools

import jax
import jax.numpy as jnp
from jax import lax
from jax.experimental import pallas as pl
from jax.experimental.pallas import tpu as pltpu
from jax.sharding import PartitionSpec as P

ROWB = 4
ITERS = 2
PIECE = 2
PARAMS = pltpu.CompilerParams(vmem_limit_bytes=16 << 20)
BOTH = ("wide", "narrow")
SMEM = pl.BlockSpec(memory_space=pltpu.SMEM)
VMEM = pl.BlockSpec(memory_space=pltpu.VMEM)
HBM = pl.BlockSpec(memory_space=pltpu.HBM)


def kept(values, space):
    return [pltpu.with_memory_space_constraint(value, space) for value in values]


def raise_row(peak_ref, index, row):
    peak_ref[pl.ds(index, 1), :] = jnp.maximum(peak_ref[pl.ds(index, 1), :], row)


def lane_max(block):
    half = block.shape[1] // 2
    folded = jnp.maximum(block[:, :half], block[:, half:])
    return jnp.max(folded.T, axis=0, keepdims=True)


def as_column(row, half):
    return jnp.broadcast_to(row, (half, row.shape[1])).T


def first_kernel(
    count_ref,
    rows_in,
    cols_in,
    tiles_ref,
    rows_ref,
    cols_ref,
    peak_ref,
    places_ref,
    *refs,
):
    *held_refs, sems = refs
    slots = tiles_ref.shape[1]
    every = [ref.at[s] for ref in held_refs for s in range(ref.shape[0])]
    held, sizes = every[:slots], every[slots:]
    moves = [(rows_in, rows_ref), (cols_in, cols_ref)]
    moves += [(tiles_ref.at[0, s], held[s]) for s in range(slots)]
    copies = [
        pltpu.make_async_copy(source, target, sems.at[k])
        for k, (source, target) in enumerate(moves)
    ]
    for copy in copies:
        copy.start()
    peak_ref[...] = jnp.zeros_like(peak_ref)
    for copy in copies[:2]:
        copy.wait()
    values = [count_ref[0, 0]]
    values += [ref[0, s] for s in range(slots) for ref in (rows_ref, cols_ref)]
    lane = lax.broadcasted_iota(jnp.int32, places_ref.shape, 1)
    places = jnp.zeros(places_ref.shape, jnp.int32)
    for k, value in enumerate(values):
        places = jnp.where(lane == k, value, places)
    places_ref[...] = places.astype(jnp.float32)
    for first in range(0, slots, 2):
        found = []
        for copy in copies[2 + first : 4 + first]:
            copy.wait()
        for s in range(first, min(first + 2, slots)):
            size = jnp.abs(held[s][...])
            sizes[s][...] = size
            found.append((s, jnp.max(size, axis=0, keepdims=True), lane_max(size)))
        for s, column_max, row_max in found:
            live = s < count_ref[0, 0]
            raise_row(peak_ref, cols_ref[0, s], jnp.where(live, column_max, 0.0))
            raise_row(peak_ref, rows_ref[0, s], jnp.where(live, row_max, 0.0))


def places_kernel(index_ref, places_ref, whole_ref, sem):
    whole_ref[...] = index_ref[...].astype(jnp.int32)
    copy = pltpu.make_async_copy(whole_ref, places_ref, sem.at[0])
    copy.start()
    copy.wait()


def next_kernel(row_blocks, rows_ref, cols_ref, count_ref, mate_places, old_ref, *refs):
    *tile_refs, peak_ref, scale_ref, column_ref = refs
    tiles = [ref.at[s] for ref in tile_refs for s in range(ref.shape[0])]
    slots, tile = len(tiles) // 2, tiles[0].shape[0]
    half = tile // 2
    scale_ref[...] = lax.rsqrt(old_ref[...])
    peak_ref[...] = jnp.zeros_like(peak_ref)
    start = lax.axis_index("wide") * row_blocks
    for k in range(row_blocks):
        column_ref[k] = as_column(scale_ref[pl.ds(start + k, 1), :], half)

    def add(tiles, count, places):
        found = []
        for tile_ref, (row, col) in zip(tiles, places):
            size = tile_ref[...]
            left = scale_ref[pl.ds(row, 1), :]
            right = scale_ref[pl.ds(col, 1), :]
            row_max = lane_max(size * right) * left
            column = column_ref[row - start]
            below = jnp.concatenate(
                [
                    jnp.max(size[:, :half] * column, axis=0, keepdims=True),
                    jnp.max(size[:, half:] * column, axis=0, keepdims=True),
                ],
                axis=1,
            )
            found.append((row_max, below * right))
        for s, (row_max, column_max) in enumerate(found):
            raise_row(peak_ref, places[s][0], jnp.where(s < count, row_max, 0.0))
            raise_row(peak_ref, places[s][1], jnp.where(s < count, column_max, 0.0))

    given = [mate_places[0, k] for k in range(2 * slots + 1)]
    own = [(rows_ref[0, s], cols_ref[0, s]) for s in range(slots)]
    add(tiles[:slots], count_ref[0, 0], own)
    add(tiles[slots:], given[0], list(zip(given[1::2], given[2::2])))
    peak_ref[...] = peak_ref[...] * old_ref[...]


def last_kernel(row_blocks, rows_ref, cols_ref, count_ref, old_ref, *refs):
    *held_refs, out_ref, own_out, scale_ref, own_ref, done_ref, sems = refs
    held = [ref.at[s] for ref in held_refs for s in range(ref.shape[0])]
    slots, tile = len(held), held[0].shape[0]
    half = tile // 2
    scale_ref[...] = lax.rsqrt(old_ref[...])
    start = lax.axis_index("wide") * row_blocks
    for k in range(row_blocks):
        own_ref[pl.ds(k, 1), :] = scale_ref[pl.ds(start + k, 1), :]
    copies = [pltpu.make_async_copy(own_ref, own_out, sems.at[slots])]
    copies[0].start()
    for s in range(slots):
        live = s < count_ref[0, 0]
        left = scale_ref[pl.ds(rows_ref[0, s], 1), :]
        right = scale_ref[pl.ds(cols_ref[0, s], 1), :]
        column = as_column(left, half)
        for part in (slice(0, half), slice(half, tile)):
            scaled = held[s][:, part] * column * right[:, part]
            done_ref[s, :, part] = jnp.where(live, scaled, 0.0)
        copies.append(pltpu.make_async_copy(done_ref.at[s], out_ref.at[0, s], sems.at[s]))
        copies[-1].start()
    for copy in copies:
        copy.wait()


def given_kernel(half, given_ref, own_ref, out_ref, scale_ref, sem):
    del own_ref
    w, n = lax.axis_index("wide"), lax.axis_index("narrow")

    @pl.when((w >= half) & (n < 2))
    def _():
        scale_ref[...] = lax.rsqrt(given_ref[...])
        copy = pltpu.make_async_copy(scale_ref, out_ref, sem.at[0])
        copy.start()
        copy.wait()


def swap(values, partner, wide_size, narrow_size):
    pairs = []
    for w in range(wide_size):
        for n in range(narrow_size):
            wide, narrow = partner(w, n)
            pairs.append((w * narrow_size + n, wide * narrow_size + narrow))
    return lax.ppermute(values, BOTH, pairs)


def bits(first, last):
    while first < last:
        yield first
        first *= 2


def max_over_chips(values, wide_size, narrow_size):
    steps = [(bit, 1) for bit in bits(1, wide_size)]
    steps += [(0, bit + 1) for bit in bits(2, narrow_size)]
    for wide_bit, narrow_bit in steps:
        other = swap(
            values, lambda w, n: (w ^ wide_bit, n ^ narrow_bit), wide_size, narrow_size
        )
        values = jnp.maximum(values, other)
    return values


def window_max(values, start, window):
    old = lax.dynamic_slice_in_dim(values, start, window.shape[0], 0)
    return lax.dynamic_update_slice_in_dim(values, jnp.maximum(old, window), start, 0)


def swap_in_chip(values, places, wide_size, narrow_size):
    columns = values.shape[0] // narrow_size
    row_start = lax.axis_index("wide") * ROWB
    n = lax.axis_index("narrow")
    sent = jnp.concatenate(
        [
            lax.dynamic_slice_in_dim(values, n * columns, columns, 0),
            lax.dynamic_slice_in_dim(values, row_start, ROWB, 0),
            places,
        ]
    )
    other = swap(sent, lambda w, n: (w, n ^ 1), wide_size, narrow_size)
    values = window_max(values, (n ^ 1) * columns, other[:columns])
    return window_max(values, row_start, other[columns:-1]), other[-1:]


def windows(values, wide_size, narrow_size):
    size = 2 * values.shape[0] // narrow_size
    columns = (lax.axis_index("narrow") >> 1) * size
    rows = lax.axis_index("wide") // (2 * wide_size // narrow_size) * size
    return columns, rows, size


def max_over_users(values, wide_size, narrow_size, idle):
    columns, rows, size = windows(values, wide_size, narrow_size)
    share, group_size = wide_size // narrow_size, size // 2
    half = wide_size // 2
    w, n = lax.axis_index("wide"), lax.axis_index("narrow")
    group = w // share
    for bit in bits(1, half):
        group_start = (group if bit < share else group | 1) * group_size
        sent = jnp.concatenate(
            [
                lax.dynamic_slice_in_dim(values, columns, size, 0),
                lax.dynamic_slice_in_dim(values, group_start, group_size, 0),
            ]
        )
        other = swap(sent, lambda w, n: (w ^ bit, n ^ 1), wide_size, narrow_size)
        values = window_max(values, columns, other[:size])
        values = window_max(values, group_start, other[size:])
    by_columns = swap(
        lax.dynamic_slice_in_dim(values, columns, size, 0),
        lambda w, n: (w ^ half if n > 1 else w, n ^ 1),
        wide_size,
        narrow_size,
    )
    by_rows = swap(
        lax.dynamic_slice_in_dim(values, rows, size, 0),
        lambda w, n: (w, n ^ (3 if w < half else idle)),
        wide_size,
        narrow_size,
    )
    by_columns, by_rows = lax.optimization_barrier((by_columns, by_rows))
    merged = window_max(values, columns, by_columns)

    def rows_too():
        own = lax.dynamic_slice_in_dim(merged, w * ROWB, ROWB, 0)
        return swap(
            own, lambda w, n: (w, n ^ 1 if w < half else n ^ 3), wide_size, narrow_size
        )

    return window_max(merged, rows, by_rows), rows_too


def on_device(wide_size, narrow_size, tiles, tile_rows, tile_cols, tile_counts):
    slots, tile = tiles.shape[1], tiles.shape[2]
    blocks = ROWB * wide_size
    four = narrow_size == 4
    sizes = [min(PIECE, slots - s) for s in range(0, slots, PIECE)]
    rows, cols, part, index, *held = pl.pallas_call(
        first_kernel,
        out_shape=(
            pltpu.SMEM(tile_rows.shape, jnp.int32),
            pltpu.SMEM(tile_cols.shape, jnp.int32),
            pltpu.VMEM((blocks, tile), jnp.float32),
            pltpu.VMEM((1, tile), jnp.float32),
            *[pltpu.VMEM((size, tile, tile), jnp.float32) for size in 2 * sizes],
        ),
        in_specs=[SMEM, HBM, HBM, HBM],
        out_specs=(SMEM, SMEM, VMEM, VMEM, *[VMEM for size in 2 * sizes]),
        scratch_shapes=[pltpu.SemaphoreType.DMA((2 + slots,))],
        compiler_params=PARAMS,
        name="first_peaks",
    )(tile_counts, *kept((tile_rows, tile_cols, tiles), pltpu.HBM))
    places = (*kept((rows, cols), pltpu.SMEM), tile_counts)
    part, index = swap_in_chip(part, index, wide_size, narrow_size)
    held, magnitudes = held[: len(sizes)], held[len(sizes) :]
    part, *sent = lax.optimization_barrier((part, *magnitudes))
    mates = [swap(piece, lambda w, n: (w, n ^ 1), wide_size, narrow_size) for piece in sent]
    held = kept(held, pltpu.VMEM)
    mate_places = pl.pallas_call(
        places_kernel,
        out_shape=pltpu.SMEM(index.shape, jnp.int32),
        in_specs=[VMEM],
        out_specs=SMEM,
        scratch_shapes=[pltpu.VMEM(index.shape, jnp.int32), pltpu.SemaphoreType.DMA((1,))],
        compiler_params=PARAMS,
        name="other_places",
    )(*kept([index], pltpu.VMEM))
    places_too = (*places, *kept([mate_places], pltpu.SMEM))
    for iteration in range(1, ITERS):
        if four:
            full, _ = max_over_users(part, wide_size, narrow_size, 1)
        else:
            full = max_over_chips(part, wide_size, narrow_size)
        part = pl.pallas_call(
            functools.partial(next_kernel, ROWB),
            out_shape=pltpu.VMEM((blocks, tile), jnp.float32),
            in_specs=[SMEM] * 4 + [VMEM] * (1 + 2 * len(held)),
            out_specs=VMEM,
            scratch_shapes=[
                pltpu.VMEM((blocks, tile), jnp.float32),
                pltpu.VMEM((ROWB, tile, tile // 2), jnp.float32),
            ],
            compiler_params=PARAMS,
            name="next_peaks",
        )(*places_too, *kept([full, *magnitudes, *mates], pltpu.VMEM))
    if four:
        full, rows_too = max_over_users(part, wide_size, narrow_size, 3)
    else:
        full = max_over_chips(part, wide_size, narrow_size)
    own_shape = jax.ShapeDtypeStruct((ROWB, tile), jnp.float32)
    result, own = pl.pallas_call(
        functools.partial(last_kernel, ROWB),
        out_shape=(jax.ShapeDtypeStruct(tiles.shape, jnp.float32), own_shape),
        in_specs=[SMEM] * 3 + [VMEM] * (1 + len(held)),
        out_specs=(HBM, HBM),
        scratch_shapes=[
            pltpu.VMEM((blocks, tile), jnp.float32),
            pltpu.VMEM((ROWB, tile), jnp.float32),
            pltpu.VMEM((slots, tile, tile), jnp.float32),
            pltpu.SemaphoreType.DMA((slots + 1,)),
        ],
        cost_estimate=pl.CostEstimate(
            flops=2 * tiles.size, bytes_accessed=8 * tiles.size, transcendentals=0
        ),
        compiler_params=PARAMS,
        name="scaled_tiles",
    )(*places, *kept([full], pltpu.VMEM), *held)
    if four:
        own = pl.pallas_call(
            functools.partial(given_kernel, wide_size // 2),
            out_shape=own_shape,
            in_specs=[VMEM, HBM],
            out_specs=HBM,
            scratch_shapes=[
                pltpu.VMEM((ROWB, tile), jnp.float32),
                pltpu.SemaphoreType.DMA((1,)),
            ],
            input_output_aliases={1: 0},
            compiler_params=PARAMS,
            name="given_scaling",
        )(*kept([rows_too()], pltpu.VMEM), own)
    return result, own


def solution(mesh):
    wide_size, narrow_size = mesh.shape["wide"], mesh.shape["narrow"]
    placed = (
        P("wide", "narrow", None, None),
        P("wide", "narrow"),
        P("wide", "narrow"),
        P("wide", "narrow"),
    )
    return jax.shard_map(
        functools.partial(on_device, wide_size, narrow_size),
        mesh=mesh,
        in_specs=placed,
        out_specs=(P("wide", "narrow", None, None), P("wide", None)),
        check_vma=False,
    )
```

```python
import functools

import jax
import jax.numpy as jnp
from jax import lax
from jax.experimental import pallas as pl
from jax.experimental.pallas import tpu as pltpu
from jax.sharding import PartitionSpec as P

ROWB = 4
ITERS = 2
PIECE = 2
PARAMS = pltpu.CompilerParams(vmem_limit_bytes=16 << 20)
BOTH = ("wide", "narrow")
SMEM = pl.BlockSpec(memory_space=pltpu.SMEM)
VMEM = pl.BlockSpec(memory_space=pltpu.VMEM)
HBM = pl.BlockSpec(memory_space=pltpu.HBM)


def kept(values, space):
    return [pltpu.with_memory_space_constraint(value, space) for value in values]


def raise_row(peak_ref, index, row):
    peak_ref[pl.ds(index, 1), :] = jnp.maximum(peak_ref[pl.ds(index, 1), :], row)


def lane_max(block):
    half = block.shape[1] // 2
    folded = jnp.maximum(block[:, :half], block[:, half:])
    return jnp.max(folded.T, axis=0, keepdims=True)


def as_column(row, half):
    return jnp.broadcast_to(row, (half, row.shape[1])).T


def first_kernel(
    count_ref,
    rows_in,
    cols_in,
    tiles_ref,
    rows_ref,
    cols_ref,
    peak_ref,
    places_ref,
    *refs,
):
    *held_refs, sems = refs
    slots = tiles_ref.shape[1]
    every = [ref.at[s] for ref in held_refs for s in range(ref.shape[0])]
    held, sizes = every[:slots], every[slots:]
    moves = [(rows_in, rows_ref), (cols_in, cols_ref)]
    moves += [(tiles_ref.at[0, s], held[s]) for s in range(slots)]
    copies = [
        pltpu.make_async_copy(source, target, sems.at[k])
        for k, (source, target) in enumerate(moves)
    ]
    for copy in copies:
        copy.start()
    peak_ref[...] = jnp.zeros_like(peak_ref)
    for copy in copies[:2]:
        copy.wait()
    values = [count_ref[0, 0]]
    values += [ref[0, s] for s in range(slots) for ref in (rows_ref, cols_ref)]
    lane = lax.broadcasted_iota(jnp.int32, places_ref.shape, 1)
    places = jnp.zeros(places_ref.shape, jnp.int32)
    for k, value in enumerate(values):
        places = jnp.where(lane == k, value, places)
    places_ref[...] = places.astype(jnp.float32)
    for first in range(0, slots, 2):
        found = []
        for copy in copies[2 + first : 4 + first]:
            copy.wait()
        for s in range(first, min(first + 2, slots)):
            size = jnp.abs(held[s][...])
            sizes[s][...] = size
            found.append((s, jnp.max(size, axis=0, keepdims=True), lane_max(size)))
        for s, column_max, row_max in found:
            live = s < count_ref[0, 0]
            raise_row(peak_ref, cols_ref[0, s], jnp.where(live, column_max, 0.0))
            raise_row(peak_ref, rows_ref[0, s], jnp.where(live, row_max, 0.0))


def places_kernel(index_ref, places_ref, whole_ref, sem):
    whole_ref[...] = index_ref[...].astype(jnp.int32)
    copy = pltpu.make_async_copy(whole_ref, places_ref, sem.at[0])
    copy.start()
    copy.wait()


def next_kernel(row_blocks, narrow_size, share, rows_ref, cols_ref, count_ref, mate_places, old_ref, *refs):
    *tile_refs, peak_ref, sent_ref, scale_ref, column_ref = refs
    tiles = [ref.at[s] for ref in tile_refs for s in range(ref.shape[0])]
    slots, tile = len(tiles) // 2, tiles[0].shape[0]
    half = tile // 2
    scale_ref[...] = lax.rsqrt(old_ref[...])
    peak_ref[...] = jnp.zeros_like(peak_ref)
    start = lax.axis_index("wide") * row_blocks
    for k in range(row_blocks):
        column_ref[k] = as_column(scale_ref[pl.ds(start + k, 1), :], half)

    def add(tiles, count, places):
        found = []
        for tile_ref, (row, col) in zip(tiles, places):
            size = tile_ref[...]
            left = scale_ref[pl.ds(row, 1), :]
            right = scale_ref[pl.ds(col, 1), :]
            row_max = lane_max(size * right) * left
            column = column_ref[row - start]
            below = jnp.concatenate(
                [
                    jnp.max(size[:, :half] * column, axis=0, keepdims=True),
                    jnp.max(size[:, half:] * column, axis=0, keepdims=True),
                ],
                axis=1,
            )
            found.append((row_max, below * right))
        for s, (row_max, column_max) in enumerate(found):
            raise_row(peak_ref, places[s][0], jnp.where(s < count, row_max, 0.0))
            raise_row(peak_ref, places[s][1], jnp.where(s < count, column_max, 0.0))

    given = [mate_places[0, k] for k in range(2 * slots + 1)]
    own = [(rows_ref[0, s], cols_ref[0, s]) for s in range(slots)]
    add(tiles[:slots], count_ref[0, 0], own)
    add(tiles[slots:], given[0], list(zip(given[1::2], given[2::2])))
    peak_ref[...] = peak_ref[...] * old_ref[...]
    group = peak_ref.shape[0] // narrow_size
    columns = pl.multiple_of((lax.axis_index("narrow") // 2) * 2 * group, group)
    rows = pl.multiple_of((lax.axis_index("wide") // share) * group, group)
    sent_ref[: 2 * group] = peak_ref[pl.ds(columns, 2 * group), :]
    sent_ref[2 * group :] = peak_ref[pl.ds(rows, group), :]


def last_kernel(row_blocks, rows_ref, cols_ref, count_ref, old_ref, *refs):
    *held_refs, out_ref, own_out, scale_ref, own_ref, done_ref, sems = refs
    held = [ref.at[s] for ref in held_refs for s in range(ref.shape[0])]
    slots, tile = len(held), held[0].shape[0]
    half = tile // 2
    scale_ref[...] = lax.rsqrt(old_ref[...])
    start = lax.axis_index("wide") * row_blocks
    for k in range(row_blocks):
        own_ref[pl.ds(k, 1), :] = scale_ref[pl.ds(start + k, 1), :]
    copies = [pltpu.make_async_copy(own_ref, own_out, sems.at[slots])]
    copies[0].start()
    for s in range(slots):
        live = s < count_ref[0, 0]
        left = scale_ref[pl.ds(rows_ref[0, s], 1), :]
        right = scale_ref[pl.ds(cols_ref[0, s], 1), :]
        column = as_column(left, half)
        for part in (slice(0, half), slice(half, tile)):
            scaled = held[s][:, part] * column * right[:, part]
            done_ref[s, :, part] = jnp.where(live, scaled, 0.0)
        copies.append(pltpu.make_async_copy(done_ref.at[s], out_ref.at[0, s], sems.at[s]))
        copies[-1].start()
    for copy in copies:
        copy.wait()


def given_kernel(half, given_ref, own_ref, out_ref, scale_ref, sem):
    del own_ref
    w, n = lax.axis_index("wide"), lax.axis_index("narrow")

    @pl.when((w >= half) & (n < 2))
    def _():
        scale_ref[...] = lax.rsqrt(given_ref[...])
        copy = pltpu.make_async_copy(scale_ref, out_ref, sem.at[0])
        copy.start()
        copy.wait()


def swap(values, partner, wide_size, narrow_size):
    pairs = []
    for w in range(wide_size):
        for n in range(narrow_size):
            wide, narrow = partner(w, n)
            pairs.append((w * narrow_size + n, wide * narrow_size + narrow))
    return lax.ppermute(values, BOTH, pairs)


def bits(first, last):
    while first < last:
        yield first
        first *= 2


def max_over_chips(values, wide_size, narrow_size):
    steps = [(bit, 1) for bit in bits(1, wide_size)]
    steps += [(0, bit + 1) for bit in bits(2, narrow_size)]
    for wide_bit, narrow_bit in steps:
        other = swap(
            values, lambda w, n: (w ^ wide_bit, n ^ narrow_bit), wide_size, narrow_size
        )
        values = jnp.maximum(values, other)
    return values


def window_max(values, start, window):
    old = lax.dynamic_slice_in_dim(values, start, window.shape[0], 0)
    return lax.dynamic_update_slice_in_dim(values, jnp.maximum(old, window), start, 0)


def swap_in_chip(values, places, wide_size, narrow_size):
    columns = values.shape[0] // narrow_size
    row_start = lax.axis_index("wide") * ROWB
    n = lax.axis_index("narrow")
    sent = jnp.concatenate(
        [
            lax.dynamic_slice_in_dim(values, n * columns, columns, 0),
            lax.dynamic_slice_in_dim(values, row_start, ROWB, 0),
            places,
        ]
    )
    other = swap(sent, lambda w, n: (w, n ^ 1), wide_size, narrow_size)
    values = window_max(values, (n ^ 1) * columns, other[:columns])
    return window_max(values, row_start, other[columns:-1]), other[-1:]


def windows(values, wide_size, narrow_size):
    size = 2 * values.shape[0] // narrow_size
    columns = (lax.axis_index("narrow") >> 1) * size
    rows = lax.axis_index("wide") // (2 * wide_size // narrow_size) * size
    return columns, rows, size


def max_over_users(values, wide_size, narrow_size, idle, ready=None):
    columns, rows, size = windows(values, wide_size, narrow_size)
    share, group_size = wide_size // narrow_size, size // 2
    half = wide_size // 2
    w, n = lax.axis_index("wide"), lax.axis_index("narrow")
    group = w // share
    for bit in bits(1, half):
        group_start = (group if bit < share else group | 1) * group_size
        sent = jnp.concatenate(
            [
                lax.dynamic_slice_in_dim(values, columns, size, 0),
                lax.dynamic_slice_in_dim(values, group_start, group_size, 0),
            ]
        )
        if bit == 1 and ready is not None:
            sent = ready
        other = swap(sent, lambda w, n: (w ^ bit, n ^ 1), wide_size, narrow_size)
        values = window_max(values, columns, other[:size])
        values = window_max(values, group_start, other[size:])
    by_columns = swap(
        lax.dynamic_slice_in_dim(values, columns, size, 0),
        lambda w, n: (w ^ half if n > 1 else w, n ^ 1),
        wide_size,
        narrow_size,
    )
    by_rows = swap(
        lax.dynamic_slice_in_dim(values, rows, size, 0),
        lambda w, n: (w, n ^ (3 if w < half else idle)),
        wide_size,
        narrow_size,
    )
    by_columns, by_rows = lax.optimization_barrier((by_columns, by_rows))
    merged = window_max(values, columns, by_columns)

    def rows_too():
        own = lax.dynamic_slice_in_dim(merged, w * ROWB, ROWB, 0)
        return swap(
            own, lambda w, n: (w, n ^ 1 if w < half else n ^ 3), wide_size, narrow_size
        )

    return window_max(merged, rows, by_rows), rows_too


def on_device(wide_size, narrow_size, tiles, tile_rows, tile_cols, tile_counts):
    slots, tile = tiles.shape[1], tiles.shape[2]
    blocks = ROWB * wide_size
    four = narrow_size == 4
    sizes = [min(PIECE, slots - s) for s in range(0, slots, PIECE)]
    rows, cols, part, index, *held = pl.pallas_call(
        first_kernel,
        out_shape=(
            pltpu.SMEM(tile_rows.shape, jnp.int32),
            pltpu.SMEM(tile_cols.shape, jnp.int32),
            pltpu.VMEM((blocks, tile), jnp.float32),
            pltpu.VMEM((1, tile), jnp.float32),
            *[pltpu.VMEM((size, tile, tile), jnp.float32) for size in 2 * sizes],
        ),
        in_specs=[SMEM, HBM, HBM, HBM],
        out_specs=(SMEM, SMEM, VMEM, VMEM, *[VMEM for size in 2 * sizes]),
        scratch_shapes=[pltpu.SemaphoreType.DMA((2 + slots,))],
        compiler_params=PARAMS,
        name="first_peaks",
    )(tile_counts, *kept((tile_rows, tile_cols, tiles), pltpu.HBM))
    places = (*kept((rows, cols), pltpu.SMEM), tile_counts)
    part, index = swap_in_chip(part, index, wide_size, narrow_size)
    held, magnitudes = held[: len(sizes)], held[len(sizes) :]
    part, *sent = lax.optimization_barrier((part, *magnitudes))
    mates = [swap(piece, lambda w, n: (w, n ^ 1), wide_size, narrow_size) for piece in sent]
    held = kept(held, pltpu.VMEM)
    mate_places = pl.pallas_call(
        places_kernel,
        out_shape=pltpu.SMEM(index.shape, jnp.int32),
        in_specs=[VMEM],
        out_specs=SMEM,
        scratch_shapes=[pltpu.VMEM(index.shape, jnp.int32), pltpu.SemaphoreType.DMA((1,))],
        compiler_params=PARAMS,
        name="other_places",
    )(*kept([index], pltpu.VMEM))
    places_too = (*places, *kept([mate_places], pltpu.SMEM))
    for iteration in range(1, ITERS):
        if four:
            full, _ = max_over_users(part, wide_size, narrow_size, 1)
        else:
            full = max_over_chips(part, wide_size, narrow_size)
        part, ready = pl.pallas_call(
            functools.partial(next_kernel, ROWB, narrow_size, wide_size // narrow_size),
            out_shape=(
                pltpu.VMEM((blocks, tile), jnp.float32),
                pltpu.VMEM((3 * blocks // narrow_size, tile), jnp.float32),
            ),
            in_specs=[SMEM] * 4 + [VMEM] * (1 + 2 * len(held)),
            out_specs=(VMEM, VMEM),
            scratch_shapes=[
                pltpu.VMEM((blocks, tile), jnp.float32),
                pltpu.VMEM((ROWB, tile, tile // 2), jnp.float32),
            ],
            compiler_params=PARAMS,
            name="next_peaks",
        )(*places_too, *kept([full, *magnitudes, *mates], pltpu.VMEM))
    if four:
        full, rows_too = max_over_users(part, wide_size, narrow_size, 3, ready)
    else:
        full = max_over_chips(part, wide_size, narrow_size)
    own_shape = jax.ShapeDtypeStruct((ROWB, tile), jnp.float32)
    result, own = pl.pallas_call(
        functools.partial(last_kernel, ROWB),
        out_shape=(jax.ShapeDtypeStruct(tiles.shape, jnp.float32), own_shape),
        in_specs=[SMEM] * 3 + [VMEM] * (1 + len(held)),
        out_specs=(HBM, HBM),
        scratch_shapes=[
            pltpu.VMEM((blocks, tile), jnp.float32),
            pltpu.VMEM((ROWB, tile), jnp.float32),
            pltpu.VMEM((slots, tile, tile), jnp.float32),
            pltpu.SemaphoreType.DMA((slots + 1,)),
        ],
        cost_estimate=pl.CostEstimate(
            flops=2 * tiles.size, bytes_accessed=8 * tiles.size, transcendentals=0
        ),
        compiler_params=PARAMS,
        name="scaled_tiles",
    )(*places, *kept([full], pltpu.VMEM), *held)
    if four:
        own = pl.pallas_call(
            functools.partial(given_kernel, wide_size // 2),
            out_shape=own_shape,
            in_specs=[VMEM, HBM],
            out_specs=HBM,
            scratch_shapes=[
                pltpu.VMEM((ROWB, tile), jnp.float32),
                pltpu.SemaphoreType.DMA((1,)),
            ],
            input_output_aliases={1: 0},
            compiler_params=PARAMS,
            name="given_scaling",
        )(*kept([rows_too()], pltpu.VMEM), own)
    return result, own


def solution(mesh):
    wide_size, narrow_size = mesh.shape["wide"], mesh.shape["narrow"]
    placed = (
        P("wide", "narrow", None, None),
        P("wide", "narrow"),
        P("wide", "narrow"),
        P("wide", "narrow"),
    )
    return jax.shard_map(
        functools.partial(on_device, wide_size, narrow_size),
        mesh=mesh,
        in_specs=placed,
        out_specs=(P("wide", "narrow", None, None), P("wide", None)),
        check_vma=False,
    )
```
